32 devices in a mesh: batch: 8 (over y, x, core), ctx: 4 (over z).
Axes of the slice: x: 2, y: 2, z: 4, core: 2. Of those that a mesh axis runs over, the one named last changes fastest.
Arguments:
- hidden_in: bfloat16 [8, 1024, 2048], P('batch', 'ctx'), may hold values from -6 to 6
- positions: int32 [8, 1024], P('batch', 'ctx'), may hold values from 0 to 1023, as said below
- norm1_gain: bfloat16 [2048], P(('batch', 'ctx')), may hold values from 0.25 to 1.75
- norm1_bias: bfloat16 [2048], P(('batch', 'ctx')), may hold values from -3 to 3
- w_qkv: bfloat16 [2048, 6144], P(('batch', 'ctx')), may hold values from -0.125 to 0.125
- b_qkv: bfloat16 [6144], P(('batch', 'ctx')), may hold values from -3 to 3
- w_out: bfloat16 [2048, 2048], P(('batch', 'ctx')), may hold values from -1 to 1
- norm2_gain: bfloat16 [2048], P(('batch', 'ctx')), may hold values from 0.25 to 1.75
- norm2_bias: bfloat16 [2048], P(('batch', 'ctx')), may hold values from -3 to 3
- w_gate: bfloat16 [2048, 5632], P(('batch', 'ctx')), may hold values from -0.125 to 0.125
- w_up: bfloat16 [2048, 5632], P(('batch', 'ctx')), may hold values from -0.125 to 0.125
- w_down: bfloat16 [5632, 2048], P(('batch', 'ctx')), may hold values from -0.109375 to 0.109375
- cotangent: bfloat16 [8, 1024, 2048], P('batch', 'ctx'), may hold values from -6 to 6
Outputs:
- hidden_out: bfloat16 [8, 1024, 2048], P('batch', 'ctx')
- grad_hidden: float32 [8, 1024, 2048], P('batch', 'ctx')
- grad_norm1_gain: float32 [2048], P(('batch', 'ctx'))
- grad_norm1_bias: float32 [2048], P(('batch', 'ctx'))
- grad_w_qkv: float32 [2048, 6144], P(('batch', 'ctx'))
- grad_b_qkv: float32 [6144], P(('batch', 'ctx'))
- grad_w_out: float32 [2048, 2048], P(('batch', 'ctx'))
- grad_norm2_gain: float32 [2048], P(('batch', 'ctx'))
- grad_norm2_bias: float32 [2048], P(('batch', 'ctx'))
- grad_w_gate: float32 [2048, 5632], P(('batch', 'ctx'))
- grad_w_up: float32 [2048, 5632], P(('batch', 'ctx'))
- grad_w_down: float32 [5632, 2048], P(('batch', 'ctx'))
The draws below stay inside these ranges and needn't reach their ends.
Inputs may be any that keep to these rules, and one draw needn't show every extreme that they name: In each sequence the positions are a permutation of 0 to 1023 made of runs of 128 consecutive increasing positions; each run starts at a multiple of 128 and stands at an index that is a multiple of 128; the order of the runs is drawn from the seed.
All inputs are finite; a program needn't handle non-finite values.
Results may differ from the reference program's by a relative error of at most 0.02.
Values may be sent and summed in bfloat16 or wider, within the bound.
A program may use at most 512 MiB of HBM per device.

```python
import jax
import jax.numpy as jnp
from jax import lax

HEADS = 32
HEAD_DIM = 64
ROT = 16
FF = 5632
TOK_DEV = 256
D = 2048
SEQS = 8
LENGTH = 1024


def draw_positions(key, part):
    key = jax.random.fold_in(key, 7)
    run_length = TOK_DEV // 2
    run_count = LENGTH // run_length
    seq_keys = jax.random.split(key, SEQS)
    orders = jax.vmap(lambda one_key: jax.random.permutation(one_key, run_count))(seq_keys).astype(jnp.int32)
    offsets = jnp.arange(run_length, dtype=jnp.int32)
    placed = orders[:, :, None] * run_length + offsets[None, None, :]
    return placed.reshape(SEQS, LENGTH).astype(jnp.int32)


def raised(entries, own_key, source, target, shards_of, factor):
    owner, partner = [(jnp.arange(entries.shape[position]) // (entries.shape[position] // shards_of)).reshape([-1 if axis == position else 1 for axis in range(entries.ndim)]) for position in (source, target)]
    chosen = jax.random.permutation(own_key, shards_of)[partner]
    strong = (owner == chosen) | (owner == (partner + shards_of // 2) % shards_of)
    return jnp.where(strong, factor * entries, entries)


def level_of(own_key, dims, cuts, smallest, high):
    loudness = 1.0
    for dim, shards_of in cuts:
        draws = jax.random.uniform(jax.random.fold_in(jax.random.fold_in(own_key, 6), dim), (shards_of,), jnp.float32, smallest / len(cuts), high / len(cuts))
        loudness = loudness * jnp.repeat(jnp.exp(draws), dims[dim] // shards_of).reshape((-1,) + (1,) * (len(dims) - 1 - dim))
    return loudness


def bell_draw(stream_key, extent, scale, most, pieces=(), kind=jnp.bfloat16):
    values = scale * jax.random.normal(stream_key, extent, jnp.float32)
    if pieces:
        values = values * level_of(stream_key, extent, pieces, -0.22, 0.18)
    return jnp.clip(values, -most, most).astype(kind)


def heavy_noise(own_key, shape, width, reach, cuts, heavy, kind=jnp.bfloat16):
    array = width * jax.random.normal(own_key, shape, jnp.float32)
    if cuts:
        array = array * level_of(own_key, shape, cuts, -0.22, 0.18)
    return jnp.clip(raised(array, jax.random.fold_in(own_key, 3), *heavy), -reach, reach).astype(kind)


def setup_inputs(seed: int = 0) -> dict:
    key_of = jax.random.split(jax.random.key(seed), 14)
    return {
        "hidden_in": heavy_noise(key_of[0], (SEQS, LENGTH, D), 1.0, 6.0, ((0, 8), (1, 4)), (0, 2, 8, 2.0)),
        "positions": draw_positions(jax.random.fold_in(key_of[13], 71), 0),
        "norm1_gain": jnp.clip(1.0 + 0.15 * jax.random.normal(key_of[2], (D,), jnp.float32), 0.25, 1.75).astype(jnp.bfloat16),
        "norm1_bias": bell_draw(key_of[3], (D,), 0.5, 3.0, ((0, 32),)),
        "w_qkv": bell_draw(key_of[4], (D, 3 * D), D ** -0.5, 0.125, ((0, 32),)),
        "b_qkv": bell_draw(key_of[5], (3 * D,), 0.5, 3.0, ((0, 32),)),
        "w_out": bell_draw(key_of[6], (D, D), (D // 64) ** -0.5, 1.0, ((0, 32),)),
        "norm2_gain": jnp.clip(1.0 + 0.15 * jax.random.normal(key_of[7], (D,), jnp.float32), 0.25, 1.75).astype(jnp.bfloat16),
        "norm2_bias": bell_draw(key_of[8], (D,), 0.5, 3.0, ((0, 32),)),
        "w_gate": bell_draw(key_of[9], (D, FF), D ** -0.5, 0.125, ((0, 32),)),
        "w_up": bell_draw(key_of[10], (D, FF), D ** -0.5, 0.125, ((0, 32),)),
        "w_down": bell_draw(key_of[11], (FF, D), (FF // 2) ** -0.5, 0.109375, ((0, 32),)),
        "cotangent": heavy_noise(key_of[12], (SEQS, LENGTH, D), 1.0, 6.0, ((0, 8), (1, 4)), (0, 2, 8, 2.0)),
    }


NEGATIVE = -1e+30

@jax.custom_vjp
def low(v):
    return lax.optimization_barrier(v.astype(jnp.bfloat16)).astype(jnp.float32)

@jax.custom_vjp
def low_back(v):
    return v

def low_keep(v):
    return (low(v), None)

def low_pass(kept, grad):
    return (grad,)

def back_keep(v):
    return (v, None)

def back_low(kept, grad):
    return (low(grad),)
low.defvjp(low_keep, low_pass)
low_back.defvjp(back_keep, back_low)

def product(left_side, right_side):
    return jnp.dot(left_side, right_side, precision=lax.Precision.HIGHEST, preferred_element_type=jnp.float32)

def rotary_tables(places):
    steps_half = jnp.arange(ROT // 2, dtype=jnp.float32)
    frequency = 10000.0 ** (-2.0 * steps_half / ROT)
    angles = places.astype(jnp.float32)[:, None] * frequency[None, :]
    angles = jnp.concatenate([angles, angles], axis=1)
    row_count = places.shape[0]
    cosine = jnp.concatenate([jnp.cos(angles), jnp.ones((row_count, HEAD_DIM - ROT), jnp.float32)], axis=1)
    sine_table = jnp.concatenate([jnp.sin(angles), jnp.zeros((row_count, HEAD_DIM - ROT), jnp.float32)], axis=1)
    return (cosine[:, None, :], sine_table[:, None, :])

def rotate_half(values):
    first_part = values[..., :ROT // 2]
    second_part = values[..., ROT // 2:ROT]
    return jnp.concatenate([-second_part, first_part, jnp.zeros_like(values[..., ROT:])], axis=-1)

def apply_rotary(values, cosine, sine_table):
    return values * cosine + rotate_half(values) * sine_table

def layer_norm(tokens_in, gain, offset):
    centred = tokens_in - lax.optimization_barrier(jnp.mean(tokens_in, axis=-1, keepdims=True))
    spread = lax.optimization_barrier(jnp.mean(centred * centred, axis=-1, keepdims=True))
    return centred * lax.rsqrt(spread + 1e-05) * gain + offset

def attention(query_states, key_states, value_states, places):
    block_rows = min(512, LENGTH)
    block_count = LENGTH // block_rows

    def one_block(paired):
        query_block, place_block = paired
        scores = jnp.einsum('qhd,khd->hqk', query_block, key_states, precision=lax.Precision.HIGHEST) * 0.125
        visible = (places[None, :] <= place_block[:, None])[None]
        scores = low_back(jnp.where(visible, scores, NEGATIVE))
        shifted = scores - lax.optimization_barrier(jnp.max(scores, axis=-1, keepdims=True))
        exponent = jnp.exp(shifted)
        probabilities = exponent / lax.optimization_barrier(jnp.sum(exponent, axis=-1, keepdims=True))
        return jnp.einsum('hqk,khd->qhd', low(probabilities), value_states, precision=lax.Precision.HIGHEST)
    attended = lax.map(jax.checkpoint(one_block), (query_states.reshape(block_count, block_rows, HEADS, HEAD_DIM), places.reshape(block_count, block_rows)))
    return attended.reshape(LENGTH, D)

def sequence_layer(tokens_in, places, params):
    gain_one, bias_one, qkv_weight, qkv_bias, out_weight, gain_two, bias_two, gate_weight, up_weight, down_weight = params
    normed = low(layer_norm(tokens_in, gain_one, bias_one))
    projected = low_back(product(normed, qkv_weight) + qkv_bias)
    cosine, sine_table = rotary_tables(places)
    shaped = projected.reshape(LENGTH, 3, HEADS, HEAD_DIM)
    query_states = low(apply_rotary(shaped[:, 0], cosine, sine_table))
    key_states = low(apply_rotary(shaped[:, 1], cosine, sine_table))
    value_states = low(shaped[:, 2])
    attended = low_back(low(attention(query_states, key_states, value_states, places)))
    branch = low_back(product(attended, out_weight))
    residual = tokens_in + branch
    normed_two = low(layer_norm(residual, gain_two, bias_two))
    gate_value = low_back(product(normed_two, gate_weight))
    up_value = low_back(product(normed_two, up_weight))
    hidden = low(jax.nn.silu(gate_value) * up_value)
    return residual + low_back(product(hidden, down_weight))

def reference(hidden_in, positions, norm1_gain, norm1_bias, w_qkv, b_qkv, w_out, norm2_gain, norm2_bias, w_gate, w_up, w_down, cotangent):
    params = tuple((member.astype(jnp.float32) for member in (norm1_gain, norm1_bias, w_qkv, b_qkv, w_out, norm2_gain, norm2_bias, w_gate, w_up, w_down)))
    tokens_in = hidden_in.astype(jnp.float32)

    def forward(all_tokens, weights):

        def one_sequence(paired):
            return sequence_layer(paired[0], paired[1], weights)
        return lax.map(jax.checkpoint(one_sequence), (all_tokens, positions))
    result, pullback = jax.vjp(forward, tokens_in, params)
    grad_tokens, grad_params = pullback(cotangent.astype(jnp.float32))
    return (result.astype(jnp.bfloat16), grad_tokens, grad_params[0], grad_params[1], grad_params[2], grad_params[3], grad_params[4], grad_params[5], grad_params[6], grad_params[7], grad_params[8], grad_params[9])
```

```python
import jax
import jax.numpy as jnp
from jax import lax
from jax.sharding import PartitionSpec as P

HEADS = 32
HEAD_DIM = 64
ROT = 16
D = 2048


EPSILON = 1e-05
NEGATIVE = -1e30


def rotary_tables(places):
    steps_half = jnp.arange(ROT // 2, dtype=jnp.float32)
    frequency = 10000.0 ** (-2.0 * steps_half / ROT)
    angles = places.astype(jnp.float32)[:, None] * frequency[None, :]
    angles = jnp.concatenate([angles, angles], axis=1)
    row_count = places.shape[0]
    cosine = jnp.concatenate(
        [jnp.cos(angles), jnp.ones((row_count, HEAD_DIM - ROT), jnp.float32)], axis=1
    )
    sine_table = jnp.concatenate(
        [jnp.sin(angles), jnp.zeros((row_count, HEAD_DIM - ROT), jnp.float32)], axis=1
    )
    return (cosine[:, None, :], sine_table[:, None, :])


def rotate_half(values):
    first_part = values[..., : ROT // 2]
    second_part = values[..., ROT // 2 : ROT]
    return jnp.concatenate([-second_part, first_part, jnp.zeros_like(values[..., ROT:])], axis=-1)


def apply_rotary(values, cosine, sine_table):
    return values * cosine + rotate_half(values) * sine_table


def rotary_back(gradient, cosine, sine_table):
    return gradient * cosine - rotate_half(gradient * sine_table)


def norm_forward(tokens_in):
    centred = tokens_in - jnp.mean(tokens_in, axis=-1, keepdims=True)
    spread = jnp.mean(centred * centred, axis=-1, keepdims=True)
    inverse = lax.rsqrt(spread + EPSILON)
    return (centred * inverse, inverse)


def norm_back(gradient, gain, scaled, inverse):
    weighted = gradient * gain
    return inverse * (
        weighted
        - jnp.mean(weighted, axis=-1, keepdims=True)
        - scaled * jnp.mean(weighted * scaled, axis=-1, keepdims=True)
    )


def left_product(left_side, right_side):
    return lax.dot_general(
        left_side, right_side, (((0,), (0,)), ((), ())), preferred_element_type=jnp.float32
    )


def right_product(left_side, right_side):
    return lax.dot_general(
        left_side, right_side, (((1,), (1,)), ((), ())), preferred_element_type=jnp.float32
    )


def body(
    hidden_in,
    positions,
    norm1_gain,
    norm1_bias,
    w_qkv,
    b_qkv,
    w_out,
    norm2_gain,
    norm2_bias,
    w_gate,
    w_up,
    w_down,
    cotangent,
):
    attn_set = (
        lax.all_gather(norm1_gain, ("batch", "ctx"), axis=0, tiled=True),
        lax.all_gather(norm1_bias, ("batch", "ctx"), axis=0, tiled=True),
        lax.all_gather(w_qkv, ("batch", "ctx"), axis=0, tiled=True),
        lax.all_gather(b_qkv, ("batch", "ctx"), axis=0, tiled=True),
        lax.all_gather(w_out, ("batch", "ctx"), axis=0, tiled=True),
    )
    key_places = lax.all_gather(positions[0], "ctx", axis=0, tiled=True)
    query_places = positions[0]
    tokens_in = hidden_in[0].astype(jnp.float32)
    token_count = tokens_in.shape[0]
    gain_one = attn_set[0].astype(jnp.float32)
    scaled_one, inverse_one = norm_forward(tokens_in)
    normed_one = (scaled_one * gain_one + attn_set[1].astype(jnp.float32)).astype(jnp.bfloat16)
    projected = jnp.dot(normed_one, attn_set[2], preferred_element_type=jnp.float32) + attn_set[
        3
    ].astype(jnp.float32)
    cosine, sine_table = rotary_tables(query_places)
    shaped = projected.reshape(token_count, 3, HEADS, HEAD_DIM)
    queries = apply_rotary(shaped[:, 0], cosine, sine_table).astype(jnp.bfloat16)
    key_local = (
        apply_rotary(shaped[:, 1], cosine, sine_table).astype(jnp.bfloat16).reshape(token_count, D)
    )
    value_local = shaped[:, 2].astype(jnp.bfloat16).reshape(token_count, D)

    def piece_scores(key_piece):
        piece_rows = key_piece.shape[0]
        scores = (
            jnp.einsum(
                "qhd,khd->hqk",
                queries,
                key_piece.reshape(piece_rows, HEADS, HEAD_DIM),
                preferred_element_type=jnp.float32,
            )
            * 0.125
        )
        visible = (key_places[None, :] <= query_places[:, None])[None]
        return (jnp.where(visible, scores, NEGATIVE), visible)

    run_max = jnp.full((HEADS, token_count), NEGATIVE, jnp.float32)
    key_piece = lax.all_gather(key_local, "ctx", axis=0, tiled=True)
    value_piece = lax.all_gather(value_local, "ctx", axis=0, tiled=True)
    piece_rows = key_piece.shape[0]
    scores, visible = piece_scores(key_piece)
    new_max = jnp.maximum(run_max, jnp.max(scores, axis=-1))
    weights = jnp.where(visible, jnp.exp(scores - new_max[..., None]), 0.0)
    run_total = jnp.sum(weights, axis=-1)
    update = jnp.einsum(
        "hqk,khd->qhd",
        weights.astype(jnp.bfloat16),
        value_piece.reshape(piece_rows, HEADS, HEAD_DIM),
        preferred_element_type=jnp.float32,
    )
    accumulated = update
    run_max, run_total, accumulated = (new_max, run_total, accumulated)
    attended_full = accumulated / jnp.transpose(run_total)[..., None]
    log_total = run_max + jnp.log(run_total)
    attended_low = attended_full.reshape(token_count, D).astype(jnp.bfloat16)
    branch = jnp.dot(attended_low, attn_set[4], preferred_element_type=jnp.float32)
    residual = tokens_in + branch
    mlp_set = (
        lax.all_gather(norm2_gain, ("batch", "ctx"), axis=0, tiled=True),
        lax.all_gather(norm2_bias, ("batch", "ctx"), axis=0, tiled=True),
        lax.all_gather(w_gate, ("batch", "ctx"), axis=0, tiled=True),
        lax.all_gather(w_up, ("batch", "ctx"), axis=0, tiled=True),
        lax.all_gather(w_down, ("batch", "ctx"), axis=0, tiled=True),
    )
    scaled_two, inverse_two = norm_forward(residual)
    normed_two = (
        scaled_two * mlp_set[0].astype(jnp.float32) + mlp_set[1].astype(jnp.float32)
    ).astype(jnp.bfloat16)
    gate_value = jnp.dot(normed_two, mlp_set[2], preferred_element_type=jnp.float32)
    up_value = jnp.dot(normed_two, mlp_set[3], preferred_element_type=jnp.float32)
    sigmoid_gate = jax.nn.sigmoid(gate_value)
    activated = gate_value * sigmoid_gate
    hidden = (activated * up_value).astype(jnp.bfloat16)
    hidden_out = (
        residual + jnp.dot(hidden, mlp_set[4], preferred_element_type=jnp.float32)
    ).astype(jnp.bfloat16)
    mlp_back = (
        lax.all_gather(norm2_gain, ("batch", "ctx"), axis=0, tiled=True),
        lax.all_gather(norm2_bias, ("batch", "ctx"), axis=0, tiled=True),
        lax.all_gather(w_gate, ("batch", "ctx"), axis=0, tiled=True),
        lax.all_gather(w_up, ("batch", "ctx"), axis=0, tiled=True),
        lax.all_gather(w_down, ("batch", "ctx"), axis=0, tiled=True),
    )
    grad_output = cotangent[0].astype(jnp.float32)
    grad_mlp = grad_output.astype(jnp.bfloat16)
    grad_down = left_product(hidden, grad_mlp)
    grad_units = right_product(grad_mlp, mlp_back[4])
    grad_gate = (
        grad_units * up_value * sigmoid_gate * (1.0 + gate_value * (1.0 - sigmoid_gate))
    ).astype(jnp.bfloat16)
    grad_up = (grad_units * activated).astype(jnp.bfloat16)
    grad_gate_weight = left_product(normed_two, grad_gate)
    grad_up_weight = left_product(normed_two, grad_up)
    grad_normed_two = right_product(grad_gate, mlp_back[2]) + right_product(grad_up, mlp_back[3])
    grad_gain_two = jnp.sum(grad_normed_two * scaled_two, axis=0)
    grad_bias_two = jnp.sum(grad_normed_two, axis=0)
    grad_residual = grad_output + norm_back(
        grad_normed_two, mlp_back[0].astype(jnp.float32), scaled_two, inverse_two
    )
    mlp_shards = (
        lax.psum_scatter(grad_gain_two, ("batch", "ctx"), scatter_dimension=0, tiled=True),
        lax.psum_scatter(grad_bias_two, ("batch", "ctx"), scatter_dimension=0, tiled=True),
        lax.psum_scatter(grad_gate_weight, ("batch", "ctx"), scatter_dimension=0, tiled=True),
        lax.psum_scatter(grad_up_weight, ("batch", "ctx"), scatter_dimension=0, tiled=True),
        lax.psum_scatter(grad_down, ("batch", "ctx"), scatter_dimension=0, tiled=True),
    )
    attn_back = (
        lax.all_gather(norm1_gain, ("batch", "ctx"), axis=0, tiled=True),
        lax.all_gather(norm1_bias, ("batch", "ctx"), axis=0, tiled=True),
        lax.all_gather(w_qkv, ("batch", "ctx"), axis=0, tiled=True),
        lax.all_gather(b_qkv, ("batch", "ctx"), axis=0, tiled=True),
        lax.all_gather(w_out, ("batch", "ctx"), axis=0, tiled=True),
    )
    grad_branch = grad_residual.astype(jnp.bfloat16)
    grad_out_weight = left_product(attended_low, grad_branch)
    grad_attended = (
        right_product(grad_branch, attn_back[4])
        .astype(jnp.bfloat16)
        .reshape(token_count, HEADS, HEAD_DIM)
    )
    row_dot = jnp.transpose(jnp.sum(grad_attended.astype(jnp.float32) * attended_full, axis=-1))
    key_piece = lax.all_gather(key_local, "ctx", axis=0, tiled=True)
    value_piece = lax.all_gather(value_local, "ctx", axis=0, tiled=True)
    piece_rows = key_piece.shape[0]
    scores, visible = piece_scores(key_piece)
    probabilities = jnp.where(visible, jnp.exp(scores - log_total[..., None]), 0.0)
    value_shaped = value_piece.reshape(piece_rows, HEADS, HEAD_DIM)
    key_shaped = key_piece.reshape(piece_rows, HEADS, HEAD_DIM)
    grad_values = jnp.einsum(
        "hqk,qhd->khd",
        probabilities.astype(jnp.bfloat16),
        grad_attended,
        preferred_element_type=jnp.float32,
    )
    grad_probs = jnp.einsum(
        "qhd,khd->hqk", grad_attended, value_shaped, preferred_element_type=jnp.float32
    )
    grad_scores = (probabilities * (grad_probs - row_dot[..., None])).astype(jnp.bfloat16)
    query_grad = 0.125 * jnp.einsum(
        "hqk,khd->qhd", grad_scores, key_shaped, preferred_element_type=jnp.float32
    )
    grad_keys = 0.125 * jnp.einsum(
        "hqk,qhd->khd", grad_scores, queries, preferred_element_type=jnp.float32
    )
    piece_grad = jnp.concatenate(
        [grad_keys.reshape(piece_rows, D), grad_values.reshape(piece_rows, D)], axis=1
    )
    pair_grad = piece_grad
    query_grad, pair_grad = (query_grad, pair_grad)
    pair_local = lax.psum_scatter(
        pair_grad.astype(jnp.bfloat16), "ctx", scatter_dimension=0, tiled=True
    ).astype(jnp.float32)
    grad_query_lin = rotary_back(query_grad, cosine, sine_table)
    grad_key_lin = rotary_back(
        pair_local[:, :D].reshape(token_count, HEADS, HEAD_DIM), cosine, sine_table
    )
    grad_value_lin = pair_local[:, D:].reshape(token_count, HEADS, HEAD_DIM)
    grad_projected = (
        jnp.stack([grad_query_lin, grad_key_lin, grad_value_lin], axis=1)
        .reshape(token_count, 3 * D)
        .astype(jnp.bfloat16)
    )
    grad_qkv_weight = left_product(normed_one, grad_projected)
    grad_qkv_bias = jnp.sum(grad_projected.astype(jnp.float32), axis=0)
    grad_normed_one = right_product(grad_projected, attn_back[2])
    grad_gain_one = jnp.sum(grad_normed_one * scaled_one, axis=0)
    grad_bias_one = jnp.sum(grad_normed_one, axis=0)
    grad_tokens = grad_residual + norm_back(
        grad_normed_one, attn_back[0].astype(jnp.float32), scaled_one, inverse_one
    )
    attn_shards = (
        lax.psum_scatter(grad_gain_one, ("batch", "ctx"), scatter_dimension=0, tiled=True),
        lax.psum_scatter(grad_bias_one, ("batch", "ctx"), scatter_dimension=0, tiled=True),
        lax.psum_scatter(grad_qkv_weight, ("batch", "ctx"), scatter_dimension=0, tiled=True),
        lax.psum_scatter(grad_qkv_bias, ("batch", "ctx"), scatter_dimension=0, tiled=True),
        lax.psum_scatter(grad_out_weight, ("batch", "ctx"), scatter_dimension=0, tiled=True),
    )
    return (
        hidden_out[None],
        grad_tokens[None],
        attn_shards[0],
        attn_shards[1],
        attn_shards[2],
        attn_shards[3],
        attn_shards[4],
        mlp_shards[0],
        mlp_shards[1],
        mlp_shards[2],
        mlp_shards[3],
        mlp_shards[4],
    )

def head_major(values, members):
    rows = values.shape[0]
    return values.reshape(rows, members, HEAD_DIM)


def split_columns(weight, groups, unit):
    rows, columns = weight.shape
    pieces = weight.reshape(rows, columns // (groups * unit), groups, unit)
    return jnp.transpose(pieces, (2, 0, 1, 3)).reshape(groups, rows, columns // groups)


def join_columns(pieces, unit):
    groups, rows, columns = pieces.shape
    spread = pieces.reshape(groups, rows, columns // unit, unit)
    return jnp.transpose(spread, (1, 2, 0, 3)).reshape(rows, groups * columns)


def gather_columns(weight, groups, unit):
    pieces = lax.all_to_all(split_columns(weight, groups, unit), "ctx", 0, 0, tiled=True)
    rows, columns = pieces.shape[1], pieces.shape[2]
    whole = lax.all_gather(pieces.reshape(groups * rows, columns), "batch", axis=0, tiled=True)
    return whole


def scatter_columns(gradient, groups, unit):
    low = gradient.astype(jnp.bfloat16)
    mine = lax.psum_scatter(low, "batch", scatter_dimension=0, tiled=True)
    pieces = mine.reshape(groups, mine.shape[0] // groups, mine.shape[1])
    pieces = lax.all_to_all(pieces, "ctx", 0, 0, tiled=True)
    return join_columns(pieces, unit).astype(jnp.float32)


def gather_tokens(values):
    return lax.all_gather(values, "ctx", axis=0, tiled=True)


def scatter_tokens(partial):
    return lax.psum_scatter(
        partial.astype(jnp.bfloat16), "ctx", scatter_dimension=0, tiled=True
    ).astype(jnp.float32)


def body_tensor(
    hidden_in,
    positions,
    norm1_gain,
    norm1_bias,
    w_qkv,
    b_qkv,
    w_out,
    norm2_gain,
    norm2_bias,
    w_gate,
    w_up,
    w_down,
    cotangent,
):
    groups = lax.axis_size("ctx")
    members = HEADS // groups
    ff_unit = w_down.shape[0]
    width = members * HEAD_DIM
    place = lax.axis_index("ctx")
    small = jnp.concatenate([norm1_gain, norm1_bias, norm2_gain, norm2_bias, b_qkv])
    every = lax.all_gather(small, ("batch", "ctx"), axis=0, tiled=False)
    share = norm1_gain.shape[0]
    gain_one = every[:, :share].reshape(-1).astype(jnp.float32)
    bias_one = every[:, share : 2 * share].reshape(-1).astype(jnp.float32)
    gain_two = every[:, 2 * share : 3 * share].reshape(-1).astype(jnp.float32)
    bias_two = every[:, 3 * share : 4 * share].reshape(-1).astype(jnp.float32)
    qkv_bias = every[:, 4 * share :].reshape(3, members, groups, HEAD_DIM)
    qkv_bias = lax.dynamic_index_in_dim(qkv_bias, place, 2, keepdims=False)
    qkv_bias = qkv_bias.reshape(3 * width).astype(jnp.float32)
    places = gather_tokens(positions[0])
    cosine, sine_table = rotary_tables(places)
    visible = (places[None, :] <= places[:, None])[None]

    qkv_weight = gather_columns(w_qkv, groups, HEAD_DIM)
    out_weight = lax.all_gather(w_out, "batch", axis=0, tiled=True)
    gate_weight = gather_columns(w_gate, groups, ff_unit)
    up_weight = gather_columns(w_up, groups, ff_unit)
    down_weight = lax.all_gather(w_down, "batch", axis=0, tiled=True)

    tokens_in = hidden_in[0].astype(jnp.float32)
    scaled_one, inverse_one = norm_forward(tokens_in)
    normed_one = gather_tokens((scaled_one * gain_one + bias_one).astype(jnp.bfloat16))
    token_count = normed_one.shape[0]
    projected = jnp.dot(normed_one, qkv_weight, preferred_element_type=jnp.float32) + qkv_bias
    shaped = projected.reshape(token_count, 3, members, HEAD_DIM)
    queries = apply_rotary(shaped[:, 0], cosine, sine_table).astype(jnp.bfloat16)
    keys = apply_rotary(shaped[:, 1], cosine, sine_table).astype(jnp.bfloat16)
    values = shaped[:, 2].astype(jnp.bfloat16)

    def masked_scores():
        scores = 0.125 * jnp.einsum(
            "qhd,khd->hqk", queries, keys, preferred_element_type=jnp.float32
        )
        return jnp.where(visible, scores, NEGATIVE)

    scores = masked_scores()
    top = jnp.max(scores, axis=-1)
    weights = jnp.exp(scores - top[..., None])
    total = jnp.sum(weights, axis=-1)
    attended_full = (
        jnp.einsum(
            "hqk,khd->qhd", weights.astype(jnp.bfloat16), values, preferred_element_type=jnp.float32
        )
        / jnp.transpose(total)[..., None]
    )
    log_total = top + jnp.log(total)
    attended = attended_full.reshape(token_count, width).astype(jnp.bfloat16)
    branch = scatter_tokens(jnp.dot(attended, out_weight, preferred_element_type=jnp.float32))
    residual = tokens_in + branch

    scaled_two, inverse_two = norm_forward(residual)
    normed_two = gather_tokens((scaled_two * gain_two + bias_two).astype(jnp.bfloat16))
    gate_value = jnp.dot(normed_two, gate_weight, preferred_element_type=jnp.float32)
    up_value = jnp.dot(normed_two, up_weight, preferred_element_type=jnp.float32)
    sigmoid_gate = jax.nn.sigmoid(gate_value)
    activated = gate_value * sigmoid_gate
    hidden = (activated * up_value).astype(jnp.bfloat16)
    hidden_out = (
        residual + scatter_tokens(jnp.dot(hidden, down_weight, preferred_element_type=jnp.float32))
    ).astype(jnp.bfloat16)

    grad_output = cotangent[0].astype(jnp.float32)
    grad_mlp = gather_tokens(cotangent[0])
    grad_down = left_product(hidden, grad_mlp)
    grad_units = right_product(grad_mlp, down_weight)
    grad_gate = (
        grad_units * up_value * sigmoid_gate * (1.0 + gate_value * (1.0 - sigmoid_gate))
    ).astype(jnp.bfloat16)
    grad_up = (grad_units * activated).astype(jnp.bfloat16)
    grad_normed_two = scatter_tokens(
        right_product(grad_gate, gate_weight) + right_product(grad_up, up_weight)
    )
    grad_gate_weight = left_product(normed_two, grad_gate)
    grad_up_weight = left_product(normed_two, grad_up)
    grad_gain_two = jnp.sum(grad_normed_two * scaled_two, axis=0)
    grad_bias_two = jnp.sum(grad_normed_two, axis=0)
    grad_residual = grad_output + norm_back(grad_normed_two, gain_two, scaled_two, inverse_two)
    down_shard = lax.psum_scatter(
        grad_down.astype(jnp.bfloat16), "batch", scatter_dimension=0, tiled=True
    ).astype(jnp.float32)
    gate_shard = scatter_columns(grad_gate_weight, groups, ff_unit)
    up_shard = scatter_columns(grad_up_weight, groups, ff_unit)

    grad_branch = gather_tokens(grad_residual.astype(jnp.bfloat16))
    grad_out_weight = left_product(attended, grad_branch)
    grad_attended = (
        right_product(grad_branch, out_weight)
        .astype(jnp.bfloat16)
        .reshape(token_count, members, HEAD_DIM)
    )
    row_dot = jnp.transpose(jnp.sum(grad_attended.astype(jnp.float32) * attended_full, axis=-1))
    probabilities = jnp.exp(masked_scores() - log_total[..., None])
    grad_values = jnp.einsum(
        "hqk,qhd->khd",
        probabilities.astype(jnp.bfloat16),
        grad_attended,
        preferred_element_type=jnp.float32,
    )
    grad_probs = jnp.einsum(
        "qhd,khd->hqk", grad_attended, values, preferred_element_type=jnp.float32
    )
    grad_scores = (probabilities * (grad_probs - row_dot[..., None])).astype(jnp.bfloat16)
    grad_queries = 0.125 * jnp.einsum(
        "hqk,khd->qhd", grad_scores, keys, preferred_element_type=jnp.float32
    )
    grad_keys = 0.125 * jnp.einsum(
        "hqk,qhd->khd", grad_scores, queries, preferred_element_type=jnp.float32
    )
    grad_projected = (
        jnp.stack(
            [
                rotary_back(grad_queries, cosine, sine_table),
                rotary_back(grad_keys, cosine, sine_table),
                grad_values,
            ],
            axis=1,
        )
        .reshape(token_count, 3 * width)
        .astype(jnp.bfloat16)
    )
    grad_normed_one = scatter_tokens(right_product(grad_projected, qkv_weight))
    grad_qkv_weight = left_product(normed_one, grad_projected)
    grad_qkv_bias = jnp.sum(grad_projected.astype(jnp.float32), axis=0)
    grad_gain_one = jnp.sum(grad_normed_one * scaled_one, axis=0)
    grad_bias_one = jnp.sum(grad_normed_one, axis=0)
    grad_tokens = grad_residual + norm_back(grad_normed_one, gain_one, scaled_one, inverse_one)
    qkv_shard = scatter_columns(grad_qkv_weight, groups, HEAD_DIM)
    out_shard = lax.psum_scatter(
        grad_out_weight.astype(jnp.bfloat16), "batch", scatter_dimension=0, tiled=True
    ).astype(jnp.float32)
    wide_bias = jnp.where(
        jnp.arange(groups)[None, None, :, None] == place,
        grad_qkv_bias.reshape(3, members, 1, HEAD_DIM),
        0.0,
    )
    device_count = lax.axis_size("batch") * groups
    vectors = jnp.concatenate(
        [
            part.reshape(device_count, -1)
            for part in (grad_gain_one, grad_bias_one, grad_gain_two, grad_bias_two, wide_bias)
        ],
        axis=1,
    )
    summed = lax.psum_scatter(vectors, ("batch", "ctx"), scatter_dimension=0, tiled=True)[0]
    return (
        hidden_out[None],
        grad_tokens[None],
        summed[:share],
        summed[share : 2 * share],
        qkv_shard,
        summed[4 * share :],
        out_shard,
        summed[2 * share : 3 * share],
        summed[3 * share : 4 * share],
        gate_shard,
        up_shard,
        down_shard,
    )


def solution(mesh):
    placed = (
        P("batch", "ctx", None),
        P("batch", "ctx"),
        P(("batch", "ctx")),
        P(("batch", "ctx")),
        P(("batch", "ctx"), None),
        P(("batch", "ctx")),
        P(("batch", "ctx"), None),
        P(("batch", "ctx")),
        P(("batch", "ctx")),
        P(("batch", "ctx"), None),
        P(("batch", "ctx"), None),
        P(("batch", "ctx"), None),
        P("batch", "ctx", None),
    )
    device_count = mesh.shape["batch"] * mesh.shape["ctx"]
    whole_heads = HEADS % device_count == 0
    return jax.shard_map(
        body_tensor if whole_heads else body,
        mesh=mesh,
        in_specs=placed,
        out_specs=(
            P("batch", "ctx", None),
            P("batch", "ctx", None),
            P(("batch", "ctx")),
            P(("batch", "ctx")),
            P(("batch", "ctx"), None),
            P(("batch", "ctx")),
            P(("batch", "ctx"), None),
            P(("batch", "ctx")),
            P(("batch", "ctx")),
            P(("batch", "ctx"), None),
            P(("batch", "ctx"), None),
            P(("batch", "ctx"), None),
        ),
        check_vma=False,
    )
```

```python
import jax
import jax.numpy as jnp
from jax import lax
from jax.sharding import PartitionSpec as P

HEADS = 32
HEAD_DIM = 64
ROT = 16
D = 2048


EPSILON = 1e-05
NEGATIVE = -1e30


def rotary_tables(places):
    steps_half = jnp.arange(ROT // 2, dtype=jnp.float32)
    frequency = 10000.0 ** (-2.0 * steps_half / ROT)
    angles = places.astype(jnp.float32)[:, None] * frequency[None, :]
    angles = jnp.concatenate([angles, angles], axis=1)
    row_count = places.shape[0]
    cosine = jnp.concatenate(
        [jnp.cos(angles), jnp.ones((row_count, HEAD_DIM - ROT), jnp.float32)], axis=1
    )
    sine_table = jnp.concatenate(
        [jnp.sin(angles), jnp.zeros((row_count, HEAD_DIM - ROT), jnp.float32)], axis=1
    )
    return (cosine[:, None, :], sine_table[:, None, :])


def rotate_half(values):
    first_part = values[..., : ROT // 2]
    second_part = values[..., ROT // 2 : ROT]
    return jnp.concatenate([-second_part, first_part, jnp.zeros_like(values[..., ROT:])], axis=-1)


def apply_rotary(values, cosine, sine_table):
    return values * cosine + rotate_half(values) * sine_table


def rotary_back(gradient, cosine, sine_table):
    return gradient * cosine - rotate_half(gradient * sine_table)


def norm_forward(tokens_in):
    centred = tokens_in - jnp.mean(tokens_in, axis=-1, keepdims=True)
    spread = jnp.mean(centred * centred, axis=-1, keepdims=True)
    inverse = lax.rsqrt(spread + EPSILON)
    return (centred * inverse, inverse)


def norm_back(gradient, gain, scaled, inverse):
    weighted = gradient * gain
    return inverse * (
        weighted
        - jnp.mean(weighted, axis=-1, keepdims=True)
        - scaled * jnp.mean(weighted * scaled, axis=-1, keepdims=True)
    )


def left_product(left_side, right_side):
    return lax.dot_general(
        left_side, right_side, (((0,), (0,)), ((), ())), preferred_element_type=jnp.float32
    )


def right_product(left_side, right_side):
    return lax.dot_general(
        left_side, right_side, (((1,), (1,)), ((), ())), preferred_element_type=jnp.float32
    )


def body(
    hidden_in,
    positions,
    norm1_gain,
    norm1_bias,
    w_qkv,
    b_qkv,
    w_out,
    norm2_gain,
    norm2_bias,
    w_gate,
    w_up,
    w_down,
    cotangent,
):
    attn_set = (
        lax.all_gather(norm1_gain, ("batch", "ctx"), axis=0, tiled=True),
        lax.all_gather(norm1_bias, ("batch", "ctx"), axis=0, tiled=True),
        lax.all_gather(w_qkv, ("batch", "ctx"), axis=0, tiled=True),
        lax.all_gather(b_qkv, ("batch", "ctx"), axis=0, tiled=True),
        lax.all_gather(w_out, ("batch", "ctx"), axis=0, tiled=True),
    )
    key_places = lax.all_gather(positions[0], "ctx", axis=0, tiled=True)
    query_places = positions[0]
    tokens_in = hidden_in[0].astype(jnp.float32)
    token_count = tokens_in.shape[0]
    gain_one = attn_set[0].astype(jnp.float32)
    scaled_one, inverse_one = norm_forward(tokens_in)
    normed_one = (scaled_one * gain_one + attn_set[1].astype(jnp.float32)).astype(jnp.bfloat16)
    projected = jnp.dot(normed_one, attn_set[2], preferred_element_type=jnp.float32) + attn_set[
        3
    ].astype(jnp.float32)
    cosine, sine_table = rotary_tables(query_places)
    shaped = projected.reshape(token_count, 3, HEADS, HEAD_DIM)
    queries = apply_rotary(shaped[:, 0], cosine, sine_table).astype(jnp.bfloat16)
    key_local = (
        apply_rotary(shaped[:, 1], cosine, sine_table).astype(jnp.bfloat16).reshape(token_count, D)
    )
    value_local = shaped[:, 2].astype(jnp.bfloat16).reshape(token_count, D)

    def piece_scores(key_piece):
        piece_rows = key_piece.shape[0]
        scores = (
            jnp.einsum(
                "qhd,khd->hqk",
                queries,
                key_piece.reshape(piece_rows, HEADS, HEAD_DIM),
                preferred_element_type=jnp.float32,
            )
            * 0.125
        )
        visible = (key_places[None, :] <= query_places[:, None])[None]
        return (jnp.where(visible, scores, NEGATIVE), visible)

    run_max = jnp.full((HEADS, token_count), NEGATIVE, jnp.float32)
    key_piece = lax.all_gather(key_local, "ctx", axis=0, tiled=True)
    value_piece = lax.all_gather(value_local, "ctx", axis=0, tiled=True)
    piece_rows = key_piece.shape[0]
    scores, visible = piece_scores(key_piece)
    new_max = jnp.maximum(run_max, jnp.max(scores, axis=-1))
    weights = jnp.where(visible, jnp.exp(scores - new_max[..., None]), 0.0)
    run_total = jnp.sum(weights, axis=-1)
    update = jnp.einsum(
        "hqk,khd->qhd",
        weights.astype(jnp.bfloat16),
        value_piece.reshape(piece_rows, HEADS, HEAD_DIM),
        preferred_element_type=jnp.float32,
    )
    accumulated = update
    run_max, run_total, accumulated = (new_max, run_total, accumulated)
    attended_full = accumulated / jnp.transpose(run_total)[..., None]
    log_total = run_max + jnp.log(run_total)
    attended_low = attended_full.reshape(token_count, D).astype(jnp.bfloat16)
    branch = jnp.dot(attended_low, attn_set[4], preferred_element_type=jnp.float32)
    residual = tokens_in + branch
    mlp_set = (
        lax.all_gather(norm2_gain, ("batch", "ctx"), axis=0, tiled=True),
        lax.all_gather(norm2_bias, ("batch", "ctx"), axis=0, tiled=True),
        lax.all_gather(w_gate, ("batch", "ctx"), axis=0, tiled=True),
        lax.all_gather(w_up, ("batch", "ctx"), axis=0, tiled=True),
        lax.all_gather(w_down, ("batch", "ctx"), axis=0, tiled=True),
    )
    scaled_two, inverse_two = norm_forward(residual)
    normed_two = (
        scaled_two * mlp_set[0].astype(jnp.float32) + mlp_set[1].astype(jnp.float32)
    ).astype(jnp.bfloat16)
    gate_value = jnp.dot(normed_two, mlp_set[2], preferred_element_type=jnp.float32)
    up_value = jnp.dot(normed_two, mlp_set[3], preferred_element_type=jnp.float32)
    sigmoid_gate = jax.nn.sigmoid(gate_value)
    activated = gate_value * sigmoid_gate
    hidden = (activated * up_value).astype(jnp.bfloat16)
    hidden_out = (
        residual + jnp.dot(hidden, mlp_set[4], preferred_element_type=jnp.float32)
    ).astype(jnp.bfloat16)
    mlp_back = (
        lax.all_gather(norm2_gain, ("batch", "ctx"), axis=0, tiled=True),
        lax.all_gather(norm2_bias, ("batch", "ctx"), axis=0, tiled=True),
        lax.all_gather(w_gate, ("batch", "ctx"), axis=0, tiled=True),
        lax.all_gather(w_up, ("batch", "ctx"), axis=0, tiled=True),
        lax.all_gather(w_down, ("batch", "ctx"), axis=0, tiled=True),
    )
    grad_output = cotangent[0].astype(jnp.float32)
    grad_mlp = grad_output.astype(jnp.bfloat16)
    grad_down = left_product(hidden, grad_mlp)
    grad_units = right_product(grad_mlp, mlp_back[4])
    grad_gate = (
        grad_units * up_value * sigmoid_gate * (1.0 + gate_value * (1.0 - sigmoid_gate))
    ).astype(jnp.bfloat16)
    grad_up = (grad_units * activated).astype(jnp.bfloat16)
    grad_gate_weight = left_product(normed_two, grad_gate)
    grad_up_weight = left_product(normed_two, grad_up)
    grad_normed_two = right_product(grad_gate, mlp_back[2]) + right_product(grad_up, mlp_back[3])
    grad_gain_two = jnp.sum(grad_normed_two * scaled_two, axis=0)
    grad_bias_two = jnp.sum(grad_normed_two, axis=0)
    grad_residual = grad_output + norm_back(
        grad_normed_two, mlp_back[0].astype(jnp.float32), scaled_two, inverse_two
    )
    mlp_shards = (
        lax.psum_scatter(grad_gain_two, ("batch", "ctx"), scatter_dimension=0, tiled=True),
        lax.psum_scatter(grad_bias_two, ("batch", "ctx"), scatter_dimension=0, tiled=True),
        lax.psum_scatter(grad_gate_weight, ("batch", "ctx"), scatter_dimension=0, tiled=True),
        lax.psum_scatter(grad_up_weight, ("batch", "ctx"), scatter_dimension=0, tiled=True),
        lax.psum_scatter(grad_down, ("batch", "ctx"), scatter_dimension=0, tiled=True),
    )
    attn_back = (
        lax.all_gather(norm1_gain, ("batch", "ctx"), axis=0, tiled=True),
        lax.all_gather(norm1_bias, ("batch", "ctx"), axis=0, tiled=True),
        lax.all_gather(w_qkv, ("batch", "ctx"), axis=0, tiled=True),
        lax.all_gather(b_qkv, ("batch", "ctx"), axis=0, tiled=True),
        lax.all_gather(w_out, ("batch", "ctx"), axis=0, tiled=True),
    )
    grad_branch = grad_residual.astype(jnp.bfloat16)
    grad_out_weight = left_product(attended_low, grad_branch)
    grad_attended = (
        right_product(grad_branch, attn_back[4])
        .astype(jnp.bfloat16)
        .reshape(token_count, HEADS, HEAD_DIM)
    )
    row_dot = jnp.transpose(jnp.sum(grad_attended.astype(jnp.float32) * attended_full, axis=-1))
    key_piece = lax.all_gather(key_local, "ctx", axis=0, tiled=True)
    value_piece = lax.all_gather(value_local, "ctx", axis=0, tiled=True)
    piece_rows = key_piece.shape[0]
    scores, visible = piece_scores(key_piece)
    probabilities = jnp.where(visible, jnp.exp(scores - log_total[..., None]), 0.0)
    value_shaped = value_piece.reshape(piece_rows, HEADS, HEAD_DIM)
    key_shaped = key_piece.reshape(piece_rows, HEADS, HEAD_DIM)
    grad_values = jnp.einsum(
        "hqk,qhd->khd",
        probabilities.astype(jnp.bfloat16),
        grad_attended,
        preferred_element_type=jnp.float32,
    )
    grad_probs = jnp.einsum(
        "qhd,khd->hqk", grad_attended, value_shaped, preferred_element_type=jnp.float32
    )
    grad_scores = (probabilities * (grad_probs - row_dot[..., None])).astype(jnp.bfloat16)
    query_grad = 0.125 * jnp.einsum(
        "hqk,khd->qhd", grad_scores, key_shaped, preferred_element_type=jnp.float32
    )
    grad_keys = 0.125 * jnp.einsum(
        "hqk,qhd->khd", grad_scores, queries, preferred_element_type=jnp.float32
    )
    piece_grad = jnp.concatenate(
        [grad_keys.reshape(piece_rows, D), grad_values.reshape(piece_rows, D)], axis=1
    )
    pair_grad = piece_grad
    query_grad, pair_grad = (query_grad, pair_grad)
    pair_local = lax.psum_scatter(
        pair_grad.astype(jnp.bfloat16), "ctx", scatter_dimension=0, tiled=True
    ).astype(jnp.float32)
    grad_query_lin = rotary_back(query_grad, cosine, sine_table)
    grad_key_lin = rotary_back(
        pair_local[:, :D].reshape(token_count, HEADS, HEAD_DIM), cosine, sine_table
    )
    grad_value_lin = pair_local[:, D:].reshape(token_count, HEADS, HEAD_DIM)
    grad_projected = (
        jnp.stack([grad_query_lin, grad_key_lin, grad_value_lin], axis=1)
        .reshape(token_count, 3 * D)
        .astype(jnp.bfloat16)
    )
    grad_qkv_weight = left_product(normed_one, grad_projected)
    grad_qkv_bias = jnp.sum(grad_projected.astype(jnp.float32), axis=0)
    grad_normed_one = right_product(grad_projected, attn_back[2])
    grad_gain_one = jnp.sum(grad_normed_one * scaled_one, axis=0)
    grad_bias_one = jnp.sum(grad_normed_one, axis=0)
    grad_tokens = grad_residual + norm_back(
        grad_normed_one, attn_back[0].astype(jnp.float32), scaled_one, inverse_one
    )
    attn_shards = (
        lax.psum_scatter(grad_gain_one, ("batch", "ctx"), scatter_dimension=0, tiled=True),
        lax.psum_scatter(grad_bias_one, ("batch", "ctx"), scatter_dimension=0, tiled=True),
        lax.psum_scatter(grad_qkv_weight, ("batch", "ctx"), scatter_dimension=0, tiled=True),
        lax.psum_scatter(grad_qkv_bias, ("batch", "ctx"), scatter_dimension=0, tiled=True),
        lax.psum_scatter(grad_out_weight, ("batch", "ctx"), scatter_dimension=0, tiled=True),
    )
    return (
        hidden_out[None],
        grad_tokens[None],
        attn_shards[0],
        attn_shards[1],
        attn_shards[2],
        attn_shards[3],
        attn_shards[4],
        mlp_shards[0],
        mlp_shards[1],
        mlp_shards[2],
        mlp_shards[3],
        mlp_shards[4],
    )

def swap(values, axis, mask):
    return lax.ppermute(values, axis, [(i, i ^ mask) for i in range(lax.axis_size(axis))])


def add_low(left, right):
    return (left.astype(jnp.float32) + right.astype(jnp.float32)).astype(jnp.bfloat16)


def relative_four(parts):
    place = lax.axis_index("ctx")
    odd, high = place % 2 == 1, place // 2 == 1
    once = [jnp.where(odd, parts[j ^ 1], parts[j]) for j in range(4)]
    return [jnp.where(high, once[j ^ 2], once[j]) for j in range(4)]


def after(values, *earlier):
    return lax.optimization_barrier((values, earlier))[0]


def chain_gather(block, work=None):
    place = lax.axis_index("ctx")
    results = []

    def step(values, passed):
        if work is None:
            return passed
        results.append(work(len(results), values))
        return after(passed, results[-1])

    up1 = lax.ppermute(block, "ctx", [(0, 1), (1, 2), (2, 3)])
    down1 = lax.ppermute(block, "ctx", [(3, 2), (2, 1), (1, 0)])
    up1, down1 = step(block, (up1, down1))
    up2 = lax.ppermute(up1, "ctx", [(1, 2), (2, 3)])
    down2 = lax.ppermute(down1, "ctx", [(2, 1), (1, 0)])
    first = jnp.where(place == 0, down1, up1)
    up2, down2 = step(first, (up2, down2))
    up3 = lax.ppermute(up2, "ctx", [(2, 3)])
    down3 = lax.ppermute(down2, "ctx", [(1, 0)])
    second = jnp.where(place == 0, down2, jnp.where(place == 3, up2, down1))
    up3, down3 = step(second, (up3, down3))
    third = jnp.where(
        place == 0, down3, jnp.where(place == 1, down2, jnp.where(place == 2, up2, up3))
    )
    step(third, None)
    return [block, first, second, third], results


def chain_sources():
    place = lax.axis_index("ctx")
    first = jnp.where(place == 0, 1, place - 1)
    second = jnp.where(place < 2, 2, jnp.where(place == 2, 3, 1))
    third = jnp.where(place < 2, 3, 0)
    return [place, first, second, third]


def chain_scatter(own, first, second, third, work=None):
    place = lax.axis_index("ctx")
    results = []

    def step(passed):
        if work is None:
            return passed
        results.append(work(len(results)))
        return after(passed, results[-1])

    up = lax.ppermute(third, "ctx", [(0, 1)])
    down = lax.ppermute(third, "ctx", [(3, 2)])
    up, down = step((up, down))
    up = lax.ppermute(
        jnp.where(place == 0, second, add_low(third, up)), "ctx", [(0, 1), (1, 2)]
    )
    down = lax.ppermute(
        jnp.where(place == 3, second, add_low(third, down)), "ctx", [(3, 2), (2, 1)]
    )
    up, down = step((up, down))
    up = lax.ppermute(
        jnp.where(place == 0, first, add_low(second, up)), "ctx", [(0, 1), (1, 2), (2, 3)]
    )
    down = lax.ppermute(add_low(first, down), "ctx", [(3, 2), (2, 1), (1, 0)])
    up, down = step((up, down))
    return own + up.astype(jnp.float32) + down.astype(jnp.float32), results


def gather_small(values):
    own, place = lax.axis_index("batch"), lax.axis_index("ctx")
    every = values[None]
    for axis, mask in (("ctx", 1), ("ctx", 2), ("batch", 1), ("batch", 2), ("batch", 4)):
        every = jnp.concatenate([every, swap(every, axis, mask)], axis=0)
    index = jnp.arange(32)
    return jnp.take(every, ((index // 4) ^ own) * 4 + ((index % 4) ^ place), axis=0)


def scatter_small(vectors):
    own, place = lax.axis_index("batch"), lax.axis_index("ctx")
    index = jnp.arange(32)
    rest = jnp.take(vectors, ((index % 8) ^ own) * 4 + ((index // 8) ^ place), axis=0)
    for axis, mask in (("ctx", 2), ("ctx", 1), ("batch", 4), ("batch", 2), ("batch", 1)):
        middle = rest.shape[0] // 2
        rest = rest[:middle] + swap(rest[middle:], axis, mask)
    return rest[0]


def split_columns(weight, unit):
    rows, columns = weight.shape
    pieces = weight.reshape(rows, columns // (4 * unit), 4, unit)
    return [pieces[:, :, j].reshape(rows, columns // 4) for j in range(4)]


def join_columns(parts, unit):
    rows, columns = parts[0].shape
    spread = jnp.stack([part.reshape(rows, columns // unit, unit) for part in parts], axis=2)
    return spread.reshape(rows, 4 * columns)


def body_chain(
    hidden_in,
    positions,
    norm1_gain,
    norm1_bias,
    w_qkv,
    b_qkv,
    w_out,
    norm2_gain,
    norm2_bias,
    w_gate,
    w_up,
    w_down,
    cotangent,
):
    place = lax.axis_index("ctx")
    members = HEADS // 4
    width = members * HEAD_DIM
    share = norm1_gain.shape[0]
    ff_unit = w_down.shape[0]
    ff_part = 8 * ff_unit
    tokens = hidden_in.shape[1]

    coarse, fine = jnp.divmod(positions[0], 256)
    small = gather_small(
        jnp.concatenate(
            [norm1_gain, norm1_bias, norm2_gain, norm2_bias, b_qkv]
            + [part.astype(jnp.bfloat16) for part in (coarse, fine)]
        )
    )
    token_blocks, _ = chain_gather(hidden_in[0])
    arrived_tokens = token_blocks[3]
    kept = 4 * share + b_qkv.shape[0]
    row = lax.dynamic_slice_in_dim(small, 4 * lax.axis_index("batch"), 4, axis=0)[:, kept:]
    row = row.astype(jnp.float32).astype(jnp.int32)
    places = row[:, :tokens] * 256 + row[:, tokens:]
    places = jnp.concatenate(
        [lax.dynamic_index_in_dim(places, source, 0, keepdims=False) for source in chain_sources()]
    )
    small = small[:, :kept]
    gain_one = small[:, :share].reshape(-1).astype(jnp.float32)
    bias_one = small[:, share : 2 * share].reshape(-1).astype(jnp.float32)
    gain_two = small[:, 2 * share : 3 * share].reshape(-1).astype(jnp.float32)
    bias_two = small[:, 3 * share : 4 * share].reshape(-1).astype(jnp.float32)
    qkv_bias = small[:, 4 * share :].reshape(3, members, 4, HEAD_DIM)
    qkv_bias = lax.dynamic_index_in_dim(qkv_bias, place, 2, keepdims=False)
    qkv_bias = qkv_bias.reshape(3 * width).astype(jnp.float32)

    def exchange(pieces):
        pieces = relative_four(pieces)
        return [pieces[0]] + [swap(pieces[m], "ctx", m) for m in (1, 2, 3)]

    def gather_rows(arrived):
        rows = jnp.concatenate(relative_four(arrived), axis=0)
        return lax.all_gather(rows, "batch", axis=0, tiled=True)

    def sum_rows(gradient):
        return lax.psum_scatter(gradient, "batch", scatter_dimension=0, tiled=True)

    def exchange_back(mine):
        arrived = exchange([mine[j * share : (j + 1) * share] for j in range(4)])
        return [part.astype(jnp.float32) for part in relative_four(arrived)]

    qkv_weight = gather_rows(exchange(split_columns(w_qkv, HEAD_DIM)))
    out_weight = lax.all_gather(w_out, "batch", axis=0, tiled=True)
    down = lax.all_gather(w_down, "batch", axis=0, tiled=True)
    gate_pieces = after(
        [
            jnp.concatenate(pair, axis=1)
            for pair in zip(split_columns(w_gate, ff_unit), split_columns(w_up, ff_unit))
        ],
        arrived_tokens,
    )
    gate_pieces = exchange(gate_pieces)
    cot_own = after(cotangent[0], arrived_tokens, down)
    cot_every = lax.all_gather(cot_own, "ctx", axis=0, tiled=False)
    cot_blocks = [
        lax.dynamic_index_in_dim(cot_every, source, 0, keepdims=False)
        for source in chain_sources()
    ]

    cosine, sine_table = rotary_tables(places)
    normed_blocks, projected_blocks = [], []
    for index, block in enumerate(token_blocks):
        scaled, inverse = norm_forward(block.astype(jnp.float32))
        if index == 0:
            scaled_one, inverse_one = scaled, inverse
        normed_blocks.append((scaled * gain_one + bias_one).astype(jnp.bfloat16))
        projected_blocks.append(
            jnp.dot(normed_blocks[-1], qkv_weight, preferred_element_type=jnp.float32) + qkv_bias
        )
    projected = jnp.concatenate(projected_blocks, axis=0)
    token_count = projected.shape[0]
    shaped = projected.reshape(token_count, 3, members, HEAD_DIM)
    queries = apply_rotary(shaped[:, 0], cosine, sine_table).astype(jnp.bfloat16)
    keys = apply_rotary(shaped[:, 1], cosine, sine_table).astype(jnp.bfloat16)
    values = shaped[:, 2].astype(jnp.bfloat16)
    visible = (places[None, :] <= places[:, None])[None]

    def masked_scores():
        scores = 0.125 * jnp.einsum(
            "qhd,khd->hqk", queries, keys, preferred_element_type=jnp.float32
        )
        return jnp.where(visible, scores, NEGATIVE)

    scores = masked_scores()
    top = jnp.max(scores, axis=-1)
    weights = jnp.exp(scores - top[..., None])
    total = jnp.sum(weights, axis=-1)
    attended_full = (
        jnp.einsum(
            "hqk,khd->qhd", weights.astype(jnp.bfloat16), values, preferred_element_type=jnp.float32
        )
        / jnp.transpose(total)[..., None]
    )
    log_total = top + jnp.log(total)
    attended = attended_full.reshape(token_count, width).astype(jnp.bfloat16)
    gate_up = gather_rows(after(gate_pieces, attended))
    partial = [
        jnp.dot(
            attended[index * tokens : (index + 1) * tokens],
            out_weight,
            preferred_element_type=jnp.float32,
        )
        for index in range(4)
    ]
    branch, _ = chain_scatter(partial[0], *[part.astype(jnp.bfloat16) for part in partial[1:]])
    residual = hidden_in[0].astype(jnp.float32) + branch

    scaled_two, inverse_two = norm_forward(residual)

    def feed_forward(index, block):
        both = jnp.dot(block, gate_up, preferred_element_type=jnp.float32)
        gate_value, up_value = both[:, :ff_part], both[:, ff_part:]
        sigmoid_gate = jax.nn.sigmoid(gate_value)
        activated = gate_value * sigmoid_gate
        grad_units = right_product(cot_blocks[index], down)
        grad_gate = (
            grad_units * up_value * sigmoid_gate * (1.0 + gate_value * (1.0 - sigmoid_gate))
        )
        grad_both = jnp.concatenate([grad_gate, grad_units * activated], axis=1).astype(
            jnp.bfloat16
        )
        back = right_product(grad_both, gate_up)
        hidden = (activated * up_value).astype(jnp.bfloat16)
        return hidden, grad_both, back if index == 0 else back.astype(jnp.bfloat16)

    normed_two, results = chain_gather(
        (scaled_two * gain_two + bias_two).astype(jnp.bfloat16), feed_forward
    )
    hidden = jnp.concatenate([part[0] for part in results], axis=0)
    grad_both = jnp.concatenate([part[1] for part in results], axis=0)

    def feed_forward_rest(index):
        if index == 0:
            return left_product(hidden, jnp.concatenate(cot_blocks, axis=0)).astype(jnp.bfloat16)
        if index == 1:
            return left_product(jnp.concatenate(normed_two, axis=0), grad_both).astype(
                jnp.bfloat16
            )
        return jnp.dot(hidden, down, preferred_element_type=jnp.float32).astype(jnp.bfloat16)

    grad_normed_two, results = chain_scatter(*[part[2] for part in results], feed_forward_rest)
    grad_down, grad_gate_up, forth = results
    grad_gain_two = jnp.sum(grad_normed_two * scaled_two, axis=0)
    grad_bias_two = jnp.sum(grad_normed_two, axis=0)
    grad_residual = cotangent[0].astype(jnp.float32) + norm_back(
        grad_normed_two, gain_two, scaled_two, inverse_two
    )
    grad_down = sum_rows(grad_down)
    grad_gate_up = sum_rows(after(grad_gate_up, grad_down))

    grad_branch, grad_attended = chain_gather(
        after(grad_residual.astype(jnp.bfloat16), grad_down),
        lambda index, block: right_product(block, out_weight).astype(jnp.bfloat16),
    )
    grad_attended = after(grad_attended, grad_gate_up)
    grad_attended = jnp.concatenate(grad_attended, axis=0).reshape(
        token_count, members, HEAD_DIM
    )
    grad_out = left_product(attended, jnp.concatenate(grad_branch, axis=0)).astype(jnp.bfloat16)
    grad_out = sum_rows(after(grad_out, grad_gate_up))
    row_dot = jnp.transpose(jnp.sum(grad_attended.astype(jnp.float32) * attended_full, axis=-1))

    def attention_back(index):
        if index == 0:
            probabilities = jnp.exp(masked_scores() - log_total[..., None])
            grad_values = jnp.einsum(
                "hqk,qhd->khd",
                probabilities.astype(jnp.bfloat16),
                grad_attended,
                preferred_element_type=jnp.float32,
            )
            grad_probs = jnp.einsum(
                "qhd,khd->hqk", grad_attended, values, preferred_element_type=jnp.float32
            )
            return grad_values, (probabilities * (grad_probs - row_dot[..., None])).astype(
                jnp.bfloat16
            )
        if index == 1:
            grad_queries = 0.125 * jnp.einsum(
                "hqk,khd->qhd", steps[0][1], keys, preferred_element_type=jnp.float32
            )
            grad_keys = 0.125 * jnp.einsum(
                "hqk,qhd->khd", steps[0][1], queries, preferred_element_type=jnp.float32
            )
            return (
                jnp.stack(
                    [
                        rotary_back(grad_queries, cosine, sine_table),
                        rotary_back(grad_keys, cosine, sine_table),
                        steps[0][0],
                    ],
                    axis=1,
                )
                .reshape(token_count, 3 * width)
                .astype(jnp.bfloat16)
            )
        return [
            right_product(steps[1][block * tokens : (block + 1) * tokens], qkv_weight)
            for block in (3, 2, 1, 0)
        ]

    steps = []

    def attention_step(index):
        steps.append(attention_back(index))
        return steps[-1]

    forth = [forth[block * tokens : (block + 1) * tokens] for block in range(4)]
    forth, _ = chain_scatter(*after(forth, grad_attended), attention_step)
    hidden_out = (residual + forth).astype(jnp.bfloat16)
    grad_projected = steps[1]
    partial = steps[2][::-1]

    def attention_rest(index):
        if index == 0:
            return left_product(
                jnp.concatenate(normed_blocks, axis=0), grad_projected
            ).astype(jnp.bfloat16)
        if index == 1:
            return jnp.sum(grad_projected.astype(jnp.float32), axis=0)
        return ()

    grad_normed_one, results = chain_scatter(
        partial[0], *[part.astype(jnp.bfloat16) for part in partial[1:]], attention_rest
    )
    grad_qkv, grad_qkv_bias, _ = results
    grad_gain_one = jnp.sum(grad_normed_one * scaled_one, axis=0)
    grad_bias_one = jnp.sum(grad_normed_one, axis=0)
    grad_tokens = grad_residual + norm_back(grad_normed_one, gain_one, scaled_one, inverse_one)

    grad_qkv = sum_rows(grad_qkv)
    out_shard = grad_out.astype(jnp.float32)
    down_shard = grad_down.astype(jnp.float32)
    gate_up_shard = exchange_back(after(grad_gate_up, grad_tokens))
    gate_shard = join_columns([part[:, :ff_part] for part in gate_up_shard], ff_unit)
    up_shard = join_columns([part[:, ff_part:] for part in gate_up_shard], ff_unit)
    qkv_shard = join_columns(exchange_back(grad_qkv), HEAD_DIM)
    wide_bias = jnp.where(
        jnp.arange(4)[None, None, :, None] == place,
        grad_qkv_bias.reshape(3, members, 1, HEAD_DIM),
        0.0,
    )
    summed = scatter_small(
        jnp.concatenate(
            [
                part.reshape(32, -1)
                for part in (grad_gain_one, grad_bias_one, grad_gain_two, grad_bias_two, wide_bias)
            ],
            axis=1,
        )
    )
    return (
        hidden_out[None],
        grad_tokens[None],
        summed[:share],
        summed[share : 2 * share],
        qkv_shard,
        summed[4 * share :],
        out_shard,
        summed[2 * share : 3 * share],
        summed[3 * share : 4 * share],
        gate_shard,
        up_shard,
        down_shard,
    )


def solution(mesh):
    placed = (
        P("batch", "ctx", None),
        P("batch", "ctx"),
        P(("batch", "ctx")),
        P(("batch", "ctx")),
        P(("batch", "ctx"), None),
        P(("batch", "ctx")),
        P(("batch", "ctx"), None),
        P(("batch", "ctx")),
        P(("batch", "ctx")),
        P(("batch", "ctx"), None),
        P(("batch", "ctx"), None),
        P(("batch", "ctx"), None),
        P("batch", "ctx", None),
    )
    chain_of_four = mesh.shape["batch"] == 8 and mesh.shape["ctx"] == 4
    return jax.shard_map(
        body_chain if chain_of_four else body,
        mesh=mesh,
        in_specs=placed,
        out_specs=(
            P("batch", "ctx", None),
            P("batch", "ctx", None),
            P(("batch", "ctx")),
            P(("batch", "ctx")),
            P(("batch", "ctx"), None),
            P(("batch", "ctx")),
            P(("batch", "ctx"), None),
            P(("batch", "ctx")),
            P(("batch", "ctx")),
            P(("batch", "ctx"), None),
            P(("batch", "ctx"), None),
            P(("batch", "ctx"), None),
        ),
        check_vma=False,
    )
```

```python
import jax
import jax.numpy as jnp
from jax import lax
from jax.experimental import pallas as pl
from jax.experimental.pallas import tpu as pltpu
from jax.sharding import PartitionSpec as P

HEADS = 32
HEAD_DIM = 64
ROT = 16
D = 2048


EPSILON = 1e-05
NEGATIVE = -1e30


def rotary_tables(places):
    steps_half = jnp.arange(ROT // 2, dtype=jnp.float32)
    frequency = 10000.0 ** (-2.0 * steps_half / ROT)
    angles = places.astype(jnp.float32)[:, None] * frequency[None, :]
    angles = jnp.concatenate([angles, angles], axis=1)
    row_count = places.shape[0]
    cosine = jnp.concatenate(
        [jnp.cos(angles), jnp.ones((row_count, HEAD_DIM - ROT), jnp.float32)], axis=1
    )
    sine_table = jnp.concatenate(
        [jnp.sin(angles), jnp.zeros((row_count, HEAD_DIM - ROT), jnp.float32)], axis=1
    )
    return (cosine[:, None, :], sine_table[:, None, :])


def rotate_half(values):
    first_part = values[..., : ROT // 2]
    second_part = values[..., ROT // 2 : ROT]
    return jnp.concatenate([-second_part, first_part, jnp.zeros_like(values[..., ROT:])], axis=-1)


def apply_rotary(values, cosine, sine_table):
    return values * cosine + rotate_half(values) * sine_table


def rotary_back(gradient, cosine, sine_table):
    return gradient * cosine - rotate_half(gradient * sine_table)


def norm_forward(tokens_in):
    centred = tokens_in - jnp.mean(tokens_in, axis=-1, keepdims=True)
    spread = jnp.mean(centred * centred, axis=-1, keepdims=True)
    inverse = lax.rsqrt(spread + EPSILON)
    return (centred * inverse, inverse)


def norm_back(gradient, gain, scaled, inverse):
    weighted = gradient * gain
    return inverse * (
        weighted
        - jnp.mean(weighted, axis=-1, keepdims=True)
        - scaled * jnp.mean(weighted * scaled, axis=-1, keepdims=True)
    )


def left_product(left_side, right_side):
    return lax.dot_general(
        left_side, right_side, (((0,), (0,)), ((), ())), preferred_element_type=jnp.float32
    )


def right_product(left_side, right_side):
    return lax.dot_general(
        left_side, right_side, (((1,), (1,)), ((), ())), preferred_element_type=jnp.float32
    )


def body(
    hidden_in,
    positions,
    norm1_gain,
    norm1_bias,
    w_qkv,
    b_qkv,
    w_out,
    norm2_gain,
    norm2_bias,
    w_gate,
    w_up,
    w_down,
    cotangent,
):
    attn_set = (
        lax.all_gather(norm1_gain, ("batch", "ctx"), axis=0, tiled=True),
        lax.all_gather(norm1_bias, ("batch", "ctx"), axis=0, tiled=True),
        lax.all_gather(w_qkv, ("batch", "ctx"), axis=0, tiled=True),
        lax.all_gather(b_qkv, ("batch", "ctx"), axis=0, tiled=True),
        lax.all_gather(w_out, ("batch", "ctx"), axis=0, tiled=True),
    )
    key_places = lax.all_gather(positions[0], "ctx", axis=0, tiled=True)
    query_places = positions[0]
    tokens_in = hidden_in[0].astype(jnp.float32)
    token_count = tokens_in.shape[0]
    gain_one = attn_set[0].astype(jnp.float32)
    scaled_one, inverse_one = norm_forward(tokens_in)
    normed_one = (scaled_one * gain_one + attn_set[1].astype(jnp.float32)).astype(jnp.bfloat16)
    projected = jnp.dot(normed_one, attn_set[2], preferred_element_type=jnp.float32) + attn_set[
        3
    ].astype(jnp.float32)
    cosine, sine_table = rotary_tables(query_places)
    shaped = projected.reshape(token_count, 3, HEADS, HEAD_DIM)
    queries = apply_rotary(shaped[:, 0], cosine, sine_table).astype(jnp.bfloat16)
    key_local = (
        apply_rotary(shaped[:, 1], cosine, sine_table).astype(jnp.bfloat16).reshape(token_count, D)
    )
    value_local = shaped[:, 2].astype(jnp.bfloat16).reshape(token_count, D)

    def piece_scores(key_piece):
        piece_rows = key_piece.shape[0]
        scores = (
            jnp.einsum(
                "qhd,khd->hqk",
                queries,
                key_piece.reshape(piece_rows, HEADS, HEAD_DIM),
                preferred_element_type=jnp.float32,
            )
            * 0.125
        )
        visible = (key_places[None, :] <= query_places[:, None])[None]
        return (jnp.where(visible, scores, NEGATIVE), visible)

    run_max = jnp.full((HEADS, token_count), NEGATIVE, jnp.float32)
    key_piece = lax.all_gather(key_local, "ctx", axis=0, tiled=True)
    value_piece = lax.all_gather(value_local, "ctx", axis=0, tiled=True)
    piece_rows = key_piece.shape[0]
    scores, visible = piece_scores(key_piece)
    new_max = jnp.maximum(run_max, jnp.max(scores, axis=-1))
    weights = jnp.where(visible, jnp.exp(scores - new_max[..., None]), 0.0)
    run_total = jnp.sum(weights, axis=-1)
    update = jnp.einsum(
        "hqk,khd->qhd",
        weights.astype(jnp.bfloat16),
        value_piece.reshape(piece_rows, HEADS, HEAD_DIM),
        preferred_element_type=jnp.float32,
    )
    accumulated = update
    run_max, run_total, accumulated = (new_max, run_total, accumulated)
    attended_full = accumulated / jnp.transpose(run_total)[..., None]
    log_total = run_max + jnp.log(run_total)
    attended_low = attended_full.reshape(token_count, D).astype(jnp.bfloat16)
    branch = jnp.dot(attended_low, attn_set[4], preferred_element_type=jnp.float32)
    residual = tokens_in + branch
    mlp_set = (
        lax.all_gather(norm2_gain, ("batch", "ctx"), axis=0, tiled=True),
        lax.all_gather(norm2_bias, ("batch", "ctx"), axis=0, tiled=True),
        lax.all_gather(w_gate, ("batch", "ctx"), axis=0, tiled=True),
        lax.all_gather(w_up, ("batch", "ctx"), axis=0, tiled=True),
        lax.all_gather(w_down, ("batch", "ctx"), axis=0, tiled=True),
    )
    scaled_two, inverse_two = norm_forward(residual)
    normed_two = (
        scaled_two * mlp_set[0].astype(jnp.float32) + mlp_set[1].astype(jnp.float32)
    ).astype(jnp.bfloat16)
    gate_value = jnp.dot(normed_two, mlp_set[2], preferred_element_type=jnp.float32)
    up_value = jnp.dot(normed_two, mlp_set[3], preferred_element_type=jnp.float32)
    sigmoid_gate = jax.nn.sigmoid(gate_value)
    activated = gate_value * sigmoid_gate
    hidden = (activated * up_value).astype(jnp.bfloat16)
    hidden_out = (
        residual + jnp.dot(hidden, mlp_set[4], preferred_element_type=jnp.float32)
    ).astype(jnp.bfloat16)
    mlp_back = (
        lax.all_gather(norm2_gain, ("batch", "ctx"), axis=0, tiled=True),
        lax.all_gather(norm2_bias, ("batch", "ctx"), axis=0, tiled=True),
        lax.all_gather(w_gate, ("batch", "ctx"), axis=0, tiled=True),
        lax.all_gather(w_up, ("batch", "ctx"), axis=0, tiled=True),
        lax.all_gather(w_down, ("batch", "ctx"), axis=0, tiled=True),
    )
    grad_output = cotangent[0].astype(jnp.float32)
    grad_mlp = grad_output.astype(jnp.bfloat16)
    grad_down = left_product(hidden, grad_mlp)
    grad_units = right_product(grad_mlp, mlp_back[4])
    grad_gate = (
        grad_units * up_value * sigmoid_gate * (1.0 + gate_value * (1.0 - sigmoid_gate))
    ).astype(jnp.bfloat16)
    grad_up = (grad_units * activated).astype(jnp.bfloat16)
    grad_gate_weight = left_product(normed_two, grad_gate)
    grad_up_weight = left_product(normed_two, grad_up)
    grad_normed_two = right_product(grad_gate, mlp_back[2]) + right_product(grad_up, mlp_back[3])
    grad_gain_two = jnp.sum(grad_normed_two * scaled_two, axis=0)
    grad_bias_two = jnp.sum(grad_normed_two, axis=0)
    grad_residual = grad_output + norm_back(
        grad_normed_two, mlp_back[0].astype(jnp.float32), scaled_two, inverse_two
    )
    mlp_shards = (
        lax.psum_scatter(grad_gain_two, ("batch", "ctx"), scatter_dimension=0, tiled=True),
        lax.psum_scatter(grad_bias_two, ("batch", "ctx"), scatter_dimension=0, tiled=True),
        lax.psum_scatter(grad_gate_weight, ("batch", "ctx"), scatter_dimension=0, tiled=True),
        lax.psum_scatter(grad_up_weight, ("batch", "ctx"), scatter_dimension=0, tiled=True),
        lax.psum_scatter(grad_down, ("batch", "ctx"), scatter_dimension=0, tiled=True),
    )
    attn_back = (
        lax.all_gather(norm1_gain, ("batch", "ctx"), axis=0, tiled=True),
        lax.all_gather(norm1_bias, ("batch", "ctx"), axis=0, tiled=True),
        lax.all_gather(w_qkv, ("batch", "ctx"), axis=0, tiled=True),
        lax.all_gather(b_qkv, ("batch", "ctx"), axis=0, tiled=True),
        lax.all_gather(w_out, ("batch", "ctx"), axis=0, tiled=True),
    )
    grad_branch = grad_residual.astype(jnp.bfloat16)
    grad_out_weight = left_product(attended_low, grad_branch)
    grad_attended = (
        right_product(grad_branch, attn_back[4])
        .astype(jnp.bfloat16)
        .reshape(token_count, HEADS, HEAD_DIM)
    )
    row_dot = jnp.transpose(jnp.sum(grad_attended.astype(jnp.float32) * attended_full, axis=-1))
    key_piece = lax.all_gather(key_local, "ctx", axis=0, tiled=True)
    value_piece = lax.all_gather(value_local, "ctx", axis=0, tiled=True)
    piece_rows = key_piece.shape[0]
    scores, visible = piece_scores(key_piece)
    probabilities = jnp.where(visible, jnp.exp(scores - log_total[..., None]), 0.0)
    value_shaped = value_piece.reshape(piece_rows, HEADS, HEAD_DIM)
    key_shaped = key_piece.reshape(piece_rows, HEADS, HEAD_DIM)
    grad_values = jnp.einsum(
        "hqk,qhd->khd",
        probabilities.astype(jnp.bfloat16),
        grad_attended,
        preferred_element_type=jnp.float32,
    )
    grad_probs = jnp.einsum(
        "qhd,khd->hqk", grad_attended, value_shaped, preferred_element_type=jnp.float32
    )
    grad_scores = (probabilities * (grad_probs - row_dot[..., None])).astype(jnp.bfloat16)
    query_grad = 0.125 * jnp.einsum(
        "hqk,khd->qhd", grad_scores, key_shaped, preferred_element_type=jnp.float32
    )
    grad_keys = 0.125 * jnp.einsum(
        "hqk,qhd->khd", grad_scores, queries, preferred_element_type=jnp.float32
    )
    piece_grad = jnp.concatenate(
        [grad_keys.reshape(piece_rows, D), grad_values.reshape(piece_rows, D)], axis=1
    )
    pair_grad = piece_grad
    query_grad, pair_grad = (query_grad, pair_grad)
    pair_local = lax.psum_scatter(
        pair_grad.astype(jnp.bfloat16), "ctx", scatter_dimension=0, tiled=True
    ).astype(jnp.float32)
    grad_query_lin = rotary_back(query_grad, cosine, sine_table)
    grad_key_lin = rotary_back(
        pair_local[:, :D].reshape(token_count, HEADS, HEAD_DIM), cosine, sine_table
    )
    grad_value_lin = pair_local[:, D:].reshape(token_count, HEADS, HEAD_DIM)
    grad_projected = (
        jnp.stack([grad_query_lin, grad_key_lin, grad_value_lin], axis=1)
        .reshape(token_count, 3 * D)
        .astype(jnp.bfloat16)
    )
    grad_qkv_weight = left_product(normed_one, grad_projected)
    grad_qkv_bias = jnp.sum(grad_projected.astype(jnp.float32), axis=0)
    grad_normed_one = right_product(grad_projected, attn_back[2])
    grad_gain_one = jnp.sum(grad_normed_one * scaled_one, axis=0)
    grad_bias_one = jnp.sum(grad_normed_one, axis=0)
    grad_tokens = grad_residual + norm_back(
        grad_normed_one, attn_back[0].astype(jnp.float32), scaled_one, inverse_one
    )
    attn_shards = (
        lax.psum_scatter(grad_gain_one, ("batch", "ctx"), scatter_dimension=0, tiled=True),
        lax.psum_scatter(grad_bias_one, ("batch", "ctx"), scatter_dimension=0, tiled=True),
        lax.psum_scatter(grad_qkv_weight, ("batch", "ctx"), scatter_dimension=0, tiled=True),
        lax.psum_scatter(grad_qkv_bias, ("batch", "ctx"), scatter_dimension=0, tiled=True),
        lax.psum_scatter(grad_out_weight, ("batch", "ctx"), scatter_dimension=0, tiled=True),
    )
    return (
        hidden_out[None],
        grad_tokens[None],
        attn_shards[0],
        attn_shards[1],
        attn_shards[2],
        attn_shards[3],
        attn_shards[4],
        mlp_shards[0],
        mlp_shards[1],
        mlp_shards[2],
        mlp_shards[3],
        mlp_shards[4],
    )

RUN = 128
PAIR = 2 * HEAD_DIM
VMEM_LIMIT = 48 * 1024 * 1024


def turn(values, tables):
    cosine, sine_up, sine_down = tables
    return (
        values * cosine
        + pltpu.roll(values, ROT // 2, 1) * sine_up
        + pltpu.roll(values, PAIR - ROT // 2, 1) * sine_down
    )


def turn_back(values, tables):
    cosine, sine_up, sine_down = tables
    return (
        values * cosine
        - pltpu.roll(values, ROT // 2, 1) * sine_up
        - pltpu.roll(values, PAIR - ROT // 2, 1) * sine_down
    )


def run_rows(runs, index):
    return pl.ds(pl.multiple_of(runs[index] * RUN, RUN), RUN)


def score_block(query, keys, start):
    scores = lax.dot_general(
        query, keys, (((1,), (1,)), ((), ())), preferred_element_type=jnp.float32
    )
    row = lax.broadcasted_iota(jnp.int32, scores.shape, 0) + start
    column = lax.broadcasted_iota(jnp.int32, scores.shape, 1)
    scores = jnp.where(column <= row, scores, NEGATIVE)
    weights = jnp.exp(scores - jnp.max(scores, axis=1, keepdims=True))
    return weights, jnp.sum(weights, axis=1, keepdims=True)


def head_lanes(values, head):
    lane = lax.broadcasted_iota(jnp.int32, values.shape, 1)
    return jnp.where((lane < HEAD_DIM) == (head == 0), values, jnp.zeros_like(values))


def attention_kernel(runs, q, k, v, cosine, sine_up, sine_down, out, q_kept, k_kept, v_kept):
    length = q.shape[0]
    for index in range(length // RUN):
        rows = run_rows(runs, index)
        place = slice(index * RUN, (index + 1) * RUN)
        tables = cosine[rows, :], sine_up[rows, :], sine_down[rows, :]
        q_kept[place, :] = turn(q[rows, :], tables).astype(jnp.bfloat16)
        k_kept[place, :] = turn(k[rows, :], tables).astype(jnp.bfloat16)
        v_kept[place, :] = v[rows, :].astype(jnp.bfloat16)
    step = 2 * RUN
    for index in range(length // step):
        seen = (index + 1) * step
        query = q_kept[index * step : seen, :]
        result = 0.0
        for head in (0, 1):
            weights, total = score_block(
                head_lanes(query, head) * 0.125, k_kept[:seen, :], index * step
            )
            summed = jnp.dot(
                weights.astype(jnp.bfloat16), v_kept[:seen, :], preferred_element_type=jnp.float32
            )
            result = result + head_lanes(summed / total, head)
        result = result.astype(jnp.bfloat16)
        out[run_rows(runs, 2 * index), :] = result[:RUN]
        out[run_rows(runs, 2 * index + 1), :] = result[RUN:]


def attention_back_kernel(
    runs, q, k, v, grad, cosine, sine_up, sine_down, q_out, k_out, v_out, k_sum, v_sum
):
    length = q.shape[0]
    step = 2 * RUN
    k_sum[...] = jnp.zeros_like(k_sum)
    v_sum[...] = jnp.zeros_like(v_sum)
    for index in range(length // step):
        seen = (index + 1) * step
        query = q[index * step : seen, :]
        pair = [run_rows(runs, 2 * index), run_rows(runs, 2 * index + 1)]
        grad_rows = jnp.concatenate([grad[rows, :] for rows in pair], axis=0)
        grad_query = 0.0
        for head in (0, 1):
            query_head = head_lanes(query, head) * 0.125
            grad_head = head_lanes(grad_rows, head)
            weights, total = score_block(query_head, k[:seen, :], index * step)
            weights = weights / total
            grad_weights = lax.dot_general(
                grad_head, v[:seen, :], (((1,), (1,)), ((), ())), preferred_element_type=jnp.float32
            )
            row_dot = jnp.sum(weights * grad_weights, axis=1, keepdims=True)
            grad_scores = (weights * (grad_weights - row_dot)).astype(jnp.bfloat16)
            grad_query = grad_query + head_lanes(
                jnp.dot(grad_scores, k[:seen, :], preferred_element_type=jnp.float32), head
            )
            k_sum[:seen, :] += left_product(grad_scores, query_head)
            v_sum[:seen, :] += left_product(weights.astype(jnp.bfloat16), grad_head)
        grad_query = grad_query * 0.125
        for part, rows in enumerate(pair):
            tables = cosine[rows, :], sine_up[rows, :], sine_down[rows, :]
            q_out[rows, :] = turn_back(
                grad_query[part * RUN : (part + 1) * RUN], tables
            ).astype(jnp.bfloat16)
    for index in range(length // RUN):
        rows = run_rows(runs, index)
        place = slice(index * RUN, (index + 1) * RUN)
        tables = cosine[rows, :], sine_up[rows, :], sine_down[rows, :]
        k_out[rows, :] = turn_back(k_sum[place, :], tables).astype(jnp.bfloat16)
        v_out[rows, :] = v_sum[place, :].astype(jnp.bfloat16)


def attention_forward(runs, projected, tables, width):
    length = projected.shape[0]
    pairs = width // PAIR
    column = lambda start: pl.BlockSpec((length, PAIR), lambda i, _: (0, i + start))
    whole = pl.BlockSpec((length, PAIR), lambda i, _: (0, 0))
    shape = jax.ShapeDtypeStruct((length, width), jnp.bfloat16)
    return pl.pallas_call(
        attention_kernel,
        out_shape=[shape] * 4,
        grid_spec=pltpu.PrefetchScalarGridSpec(
            num_scalar_prefetch=1,
            grid=(pairs,),
            in_specs=[column(0), column(pairs), column(2 * pairs)] + [whole] * 3,
            out_specs=[column(0)] * 4,
        ),
        compiler_params=pltpu.CompilerParams(vmem_limit_bytes=VMEM_LIMIT),
        cost_estimate=pl.CostEstimate(
            flops=6 * length * length * width,
            bytes_accessed=20 * length * width,
            transcendentals=2 * pairs * length * length,
        ),
        name="attention_forward",
    )(runs, projected, projected, projected, *tables)


def attention_backward(runs, kept, grad, tables):
    length, width = grad.shape
    column = pl.BlockSpec((length, PAIR), lambda i, _: (0, i))
    whole = pl.BlockSpec((length, PAIR), lambda i, _: (0, 0))
    shape = jax.ShapeDtypeStruct((length, width), jnp.bfloat16)
    return pl.pallas_call(
        attention_back_kernel,
        out_shape=[shape] * 3,
        grid_spec=pltpu.PrefetchScalarGridSpec(
            num_scalar_prefetch=1,
            grid=(width // PAIR,),
            in_specs=[column] * 4 + [whole] * 3,
            out_specs=[column] * 3,
            scratch_shapes=[pltpu.VMEM((length, PAIR), jnp.float32)] * 2,
        ),
        compiler_params=pltpu.CompilerParams(vmem_limit_bytes=VMEM_LIMIT),
        cost_estimate=pl.CostEstimate(
            flops=20 * length * length * width,
            bytes_accessed=14 * length * width,
            transcendentals=2 * width // PAIR * length * length,
        ),
        name="attention_backward",
    )(runs, *kept, grad, *tables)


def pair_tables(places):
    cosine, sine_table = rotary_tables(places)
    cosine, sine_table = cosine[:, 0], sine_table[:, 0]
    first = jnp.arange(HEAD_DIM) < ROT // 2
    up = jnp.where(first, 0.0, sine_table)
    down = jnp.where(first, -sine_table, 0.0)
    return [jnp.concatenate([table, table], axis=1) for table in (cosine, up, down)]


def swap(values, axis, mask):
    return lax.ppermute(values, axis, [(i, i ^ mask) for i in range(lax.axis_size(axis))])


def add_low(left, right):
    return (left.astype(jnp.float32) + right.astype(jnp.float32)).astype(jnp.bfloat16)


def relative_four(parts):
    place = lax.axis_index("ctx")
    odd, high = place % 2 == 1, place // 2 == 1
    once = [jnp.where(odd, parts[j ^ 1], parts[j]) for j in range(4)]
    return [jnp.where(high, once[j ^ 2], once[j]) for j in range(4)]


def after(values, *earlier):
    return lax.optimization_barrier((values, earlier))[0]


def greet(place, last):
    barrier = pltpu.get_barrier_semaphore()
    for there, near in ((place > 0, place - 1), (place < last, place + 1)):

        @pl.when(there)
        def _():
            pl.semaphore_signal(
                barrier, inc=1, device_id={"ctx": near}, device_id_type=pl.DeviceIdType.MESH
            )

    peers = jnp.where(place > 0, 1, 0) + jnp.where(place < last, 1, 0)
    pl.semaphore_wait(barrier, peers)


def towards(source, target, send, receive, device):
    return pltpu.make_async_remote_copy(
        src_ref=source,
        dst_ref=target,
        send_sem=send,
        recv_sem=receive,
        device_id={"ctx": device},
        device_id_type=pl.DeviceIdType.MESH,
    )


def gather_kernel(own, out, local, send_up, receive_up, send_down, receive_down):
    place = lax.axis_index("ctx")
    last = out.shape[0] - 1
    greet(place, last)
    mine = pltpu.make_async_copy(own, out.at[place], local)
    mine.start()
    for step in range(last):
        up_from = jnp.maximum(place - step, 0)
        down_from = jnp.minimum(place + step, last)
        source_up = own if step == 0 else out.at[up_from]
        source_down = own if step == 0 else out.at[down_from]
        up = towards(
            source_up,
            out.at[up_from],
            send_up.at[step],
            receive_up.at[step],
            jnp.minimum(place + 1, last),
        )
        down = towards(
            source_down,
            out.at[down_from],
            send_down.at[step],
            receive_down.at[step],
            jnp.maximum(place - 1, 0),
        )

        @pl.when((place >= step) & (place < last))
        def _():
            up.start()

        @pl.when((place <= last - step) & (place > 0))
        def _():
            down.start()

        @pl.when(place >= step + 1)
        def _():
            up.wait_recv()

        @pl.when(place <= last - step - 1)
        def _():
            down.wait_recv()

        @pl.when((place >= step) & (place < last))
        def _():
            up.wait_send()

        @pl.when((place <= last - step) & (place > 0))
        def _():
            down.wait_send()

    mine.wait()


def gather_tokens(block, group):
    size = lax.axis_size("ctx")
    return pl.pallas_call(
        gather_kernel,
        out_shape=jax.ShapeDtypeStruct((size, *block.shape), block.dtype),
        in_specs=[pl.BlockSpec(memory_space=pl.ANY)],
        out_specs=pl.BlockSpec(memory_space=pl.ANY),
        scratch_shapes=[pltpu.SemaphoreType.DMA] + [pltpu.SemaphoreType.DMA((size - 1,))] * 4,
        compiler_params=pltpu.CompilerParams(collective_id=group, has_side_effects=True),
        cost_estimate=pl.CostEstimate(
            flops=0, bytes_accessed=500 * block.size, transcendentals=0
        ),
        name="gather_tokens",
    )(block)


def scatter_kernel(
    partial, out, sum_up, sum_down, in_up, in_down, send_up, receive_up, send_down, receive_down
):
    place = lax.axis_index("ctx")
    last = partial.shape[0] - 1
    greet(place, last)
    for step in range(last):
        up_to = jnp.minimum(place + last - step, last)
        down_to = jnp.maximum(place - last + step, 0)
        goes_up = (place <= step) & (place < last)
        goes_down = (place >= last - step) & (place > 0)

        @pl.when(goes_up)
        def _():
            sum_up[step] = partial[up_to]

        @pl.when(goes_down)
        def _():
            sum_down[step] = partial[down_to]

        if step > 0:

            @pl.when(goes_up & (place > 0))
            def _():
                sum_up[step] = add_low(sum_up[step], in_up[step - 1])

            @pl.when(goes_down & (place < last))
            def _():
                sum_down[step] = add_low(sum_down[step], in_down[step - 1])

        up = towards(
            sum_up.at[step],
            in_up.at[step],
            send_up.at[step],
            receive_up.at[step],
            jnp.minimum(place + 1, last),
        )
        down = towards(
            sum_down.at[step],
            in_down.at[step],
            send_down.at[step],
            receive_down.at[step],
            jnp.maximum(place - 1, 0),
        )

        @pl.when(goes_up)
        def _():
            up.start()

        @pl.when(goes_down)
        def _():
            down.start()

        if step == 0:
            out[...] = partial[place].astype(jnp.float32)

        @pl.when((place > 0) & (place - 1 <= step))
        def _():
            up.wait_recv()

        @pl.when((place < last) & (place + 1 >= last - step))
        def _():
            down.wait_recv()

        @pl.when(goes_up)
        def _():
            up.wait_send()

        @pl.when(goes_down)
        def _():
            down.wait_send()

    @pl.when(place > 0)
    def _():
        out[...] += in_up[last - 1].astype(jnp.float32)

    @pl.when(place < last)
    def _():
        out[...] += in_down[last - 1].astype(jnp.float32)


def scatter_tokens(partial, group):
    size = lax.axis_size("ctx")
    partial = partial.astype(jnp.bfloat16).reshape(size, -1, partial.shape[1])
    block = partial.shape[1:]
    buffer = pltpu.VMEM((size - 1, *block), jnp.bfloat16)
    return pl.pallas_call(
        scatter_kernel,
        out_shape=jax.ShapeDtypeStruct(block, jnp.float32),
        in_specs=[pl.BlockSpec(memory_space=pltpu.VMEM)],
        out_specs=pl.BlockSpec(memory_space=pltpu.VMEM),
        scratch_shapes=[buffer] * 4 + [pltpu.SemaphoreType.DMA((size - 1,))] * 4,
        compiler_params=pltpu.CompilerParams(
            collective_id=group, has_side_effects=True, vmem_limit_bytes=VMEM_LIMIT
        ),
        cost_estimate=pl.CostEstimate(
            flops=0, bytes_accessed=150 * partial.size, transcendentals=0
        ),
        name="scatter_tokens",
    )(partial)


def gather_small(values):
    every = values[None]
    for mask in (1, 2, 4):
        every = jnp.concatenate([every, swap(every, "batch", mask)], axis=0)
    return every


def scatter_small(vectors):
    own, place = lax.axis_index("batch"), lax.axis_index("ctx")
    index = jnp.arange(32)
    rest = jnp.take(vectors, ((index % 8) ^ own) * 4 + ((index // 8) ^ place), axis=0)
    for axis, mask in (("ctx", 2), ("ctx", 1), ("batch", 4), ("batch", 2), ("batch", 1)):
        middle = rest.shape[0] // 2
        rest = rest[:middle] + swap(rest[middle:], axis, mask)
    return rest[0]


def by_bit(bit, parts):
    return jnp.where(bit, parts[1], parts[0]), jnp.where(bit, parts[0], parts[1])


def quad_gather(block, between=None):
    half = block.shape[0] // 2
    from_x = swap(block, "batch", 2)
    from_z = swap(block, "ctx", 1)
    if between is not None:
        from_x, from_z = between((from_x, from_z))
    top = swap(from_z[:half], "batch", 2)
    low = swap(from_x[half:], "ctx", 1)
    return jnp.concatenate([block, from_x, from_z, top, low], axis=0)


def quad_scatter(partial, work=None):
    rows = partial.shape[0] // 4
    half = rows // 2
    low_bits = partial[rows:].astype(jnp.bfloat16)
    x_top, x_low, z_top, z_low, d_top, d_low = [
        low_bits[j * half : (j + 1) * half] for j in range(6)
    ]
    top = swap(jnp.concatenate([z_top, d_top], axis=0), "ctx", 1)
    low = swap(jnp.concatenate([x_low, d_low], axis=0), "batch", 2)
    result = None
    if work is not None:
        result = work()
        top, low = after((top, low), result)
    top_last = swap(add_low(x_top, top[half:]), "batch", 2)
    low_last = swap(add_low(z_low, low[half:]), "ctx", 1)
    first = jnp.concatenate([top[:half], low[:half]], axis=0).astype(jnp.float32)
    last = jnp.concatenate([top_last, low_last], axis=0).astype(jnp.float32)
    return partial[:rows] + first + last, result


def swap_block_order(values):
    size = values.shape[1] // 8
    order = (0, 2, 1, 3, 4, 6, 5, 7)
    return jnp.concatenate([values[:, j * size : (j + 1) * size] for j in order], axis=1)


SAME_X = [[0, 1, 4, 5], [2, 3, 6, 7]]


def split_columns(weight, unit):
    rows, columns = weight.shape
    pieces = weight.reshape(rows, columns // (4 * unit), 4, unit)
    return [pieces[:, :, j].reshape(rows, columns // 4) for j in range(4)]


def join_columns(parts, unit):
    rows, columns = parts[0].shape
    spread = jnp.stack([part.reshape(rows, columns // unit, unit) for part in parts], axis=2)
    return spread.reshape(rows, 4 * columns)


def body_chain(
    hidden_in,
    positions,
    norm1_gain,
    norm1_bias,
    w_qkv,
    b_qkv,
    w_out,
    norm2_gain,
    norm2_bias,
    w_gate,
    w_up,
    w_down,
    cotangent,
):
    place = lax.axis_index("ctx")
    members = HEADS // 4
    width = members * HEAD_DIM
    share = norm1_gain.shape[0]
    ff_unit = w_down.shape[0]
    ff_part = 8 * ff_unit
    tokens = hidden_in.shape[1]

    coarse, fine = jnp.divmod(positions[0], 256)
    small = gather_small(
        jnp.concatenate(
            [norm1_gain, norm1_bias, norm2_gain, norm2_bias, b_qkv]
            + [part.astype(jnp.bfloat16) for part in (coarse, fine)]
        )
    )
    kept_small = small.shape[1]
    extra_rows = -(-small.size // (16 * D)) * 16
    extra = jnp.pad(small.reshape(-1), (0, extra_rows * D - small.size)).reshape(-1, D)
    token_blocks = gather_tokens(jnp.concatenate([hidden_in[0], extra], axis=0), 0)
    arrived_tokens = token_blocks
    small = token_blocks[:, tokens:].reshape(4, -1)[:, : small.size].reshape(4, 8, kept_small)
    tokens_all = token_blocks[:, :tokens].reshape(4 * tokens, D)
    kept = kept_small - 2 * tokens
    places = small[:, 0, kept:].astype(jnp.float32).astype(jnp.int32)
    places = (places[:, :tokens] * 256 + places[:, tokens:]).reshape(-1)
    index = jnp.arange(32)
    index = index % 4 * 8 + ((index // 4) ^ lax.axis_index("batch"))
    small = jnp.take(small.reshape(32, kept_small), index, axis=0)[:, :kept]
    gain_one = small[:, :share].reshape(-1).astype(jnp.float32)
    bias_one = small[:, share : 2 * share].reshape(-1).astype(jnp.float32)
    gain_two = small[:, 2 * share : 3 * share].reshape(-1).astype(jnp.float32)
    bias_two = small[:, 3 * share : 4 * share].reshape(-1).astype(jnp.float32)
    qkv_bias = small[:, 4 * share :].reshape(3, members, 4, HEAD_DIM)
    qkv_bias = lax.dynamic_index_in_dim(qkv_bias, place, 2, keepdims=False)
    qkv_bias = qkv_bias.reshape(3 * width).astype(jnp.float32)

    def exchange(pieces):
        pieces = relative_four(pieces)
        return [pieces[0]] + [swap(pieces[m], "ctx", m) for m in (1, 2, 3)]

    def gather_rows(arrived):
        rows = jnp.concatenate(relative_four(arrived), axis=0)
        return lax.all_gather(rows, "batch", axis=0, tiled=True)

    def sum_rows(gradient):
        return lax.psum_scatter(gradient, "batch", scatter_dimension=0, tiled=True)

    def exchange_back(mine):
        arrived = exchange([mine[j * share : (j + 1) * share] for j in range(4)])
        return [part.astype(jnp.float32) for part in relative_four(arrived)]

    qkv_weight = gather_rows(exchange(split_columns(after(w_qkv, extra), HEAD_DIM)))
    out_weight = lax.all_gather(w_out, "batch", axis=0, tiled=True)

    x_bit = lax.axis_index("batch") // 2 % 2 == 1
    odd, high = place % 2 == 1, place // 2 == 1

    def quarter(weight, x, parity):
        units = weight.reshape(share, 2, 2, 2, 2, 2, ff_unit)
        return units[:, :, x, :, :, parity].reshape(share, ff_part)

    kept_x, sent_x = by_bit(
        x_bit,
        [
            jnp.concatenate(
                [
                    jnp.concatenate([quarter(w_gate, x, parity), quarter(w_up, x, parity)], axis=1)
                    for parity in (0, 1)
                ],
                axis=0,
            )
            for x in (0, 1)
        ],
    )
    came_x = swap(sent_x, "batch", 2)
    first_x, second_x = by_bit(x_bit, [kept_x, came_x])
    for_parity = by_bit(
        odd,
        [
            jnp.concatenate(
                [part[parity * share : (parity + 1) * share] for part in (first_x, second_x)],
                axis=0,
            )
            for parity in (0, 1)
        ],
    )
    for_parity, cot_own = after((for_parity, cotangent[0]), arrived_tokens)
    gate_pieces = [for_parity[0]] + [swap(for_parity[m % 2], "ctx", m) for m in (1, 2, 3)]
    tables = pair_tables(places)
    starts = places[::RUN] // RUN
    order = jnp.arange(starts.shape[0])
    runs = jnp.sum(jnp.where(starts[None, :] == order[:, None], order[None, :], 0), axis=1)
    runs = runs.astype(jnp.int32)
    scaled_all, inverse_all = norm_forward(tokens_all.astype(jnp.float32))
    scaled_one = lax.dynamic_slice_in_dim(scaled_all, place * tokens, tokens, axis=0)
    inverse_one = lax.dynamic_slice_in_dim(inverse_all, place * tokens, tokens, axis=0)
    normed_all = (scaled_all * gain_one + bias_one).astype(jnp.bfloat16)
    projected = jnp.dot(normed_all, qkv_weight, preferred_element_type=jnp.float32) + qkv_bias
    attended, *kept = attention_forward(runs, projected, tables, width)
    branch = scatter_tokens(jnp.dot(attended, out_weight, preferred_element_type=jnp.float32), 1)
    gate_pieces = after(gate_pieces, attended)
    down_piece = after(swap(after(w_down, gate_pieces), "ctx", 2), branch)
    cot_quad = quad_gather(cot_own, lambda passed: after(passed, attended))
    gate_pieces = relative_four(gate_pieces)
    gate_up = lax.all_gather(
        jnp.concatenate(
            [
                gate_pieces[z][x * share : (x + 1) * share]
                for x in (0, 1)
                for z in range(4)
            ],
            axis=0,
        ),
        "batch",
        axis=0,
        tiled=True,
        axis_index_groups=SAME_X,
    )
    down = lax.all_gather(
        jnp.concatenate(by_bit(high, [w_down, down_piece]), axis=0),
        "batch",
        axis=0,
        tiled=True,
        axis_index_groups=SAME_X,
    )

    residual = hidden_in[0].astype(jnp.float32) + branch

    scaled_two, inverse_two = norm_forward(residual)
    normed_quad = quad_gather(
        swap_block_order((scaled_two * gain_two + bias_two).astype(jnp.bfloat16))
    )
    both = jnp.dot(normed_quad, gate_up, preferred_element_type=jnp.float32)
    gate_value, up_value = both[:, :ff_part], both[:, ff_part:]
    sigmoid_gate = jax.nn.sigmoid(gate_value)
    activated = gate_value * sigmoid_gate
    hidden = (activated * up_value).astype(jnp.bfloat16)
    grad_units = right_product(cot_quad, down)
    grad_gate = grad_units * up_value * sigmoid_gate * (1.0 + gate_value * (1.0 - sigmoid_gate))
    grad_both = jnp.concatenate([grad_gate, grad_units * activated], axis=1).astype(jnp.bfloat16)
    grad_normed_two, grad_gate_up = quad_scatter(
        right_product(grad_both, gate_up),
        lambda: (
            left_product(hidden, cot_quad).astype(jnp.bfloat16),
            left_product(normed_quad, grad_both).astype(jnp.bfloat16),
        ),
    )
    grad_down, grad_gate_up = grad_gate_up
    grad_normed_two = swap_block_order(grad_normed_two)

    def sum_quarter(gradient):
        return lax.psum_scatter(
            gradient, "batch", scatter_dimension=0, tiled=True, axis_index_groups=SAME_X
        )

    grad_down = sum_quarter(grad_down)
    grad_gate_up = sum_quarter(grad_gate_up)
    grad_gain_two = jnp.sum(grad_normed_two * scaled_two, axis=0)
    grad_bias_two = jnp.sum(grad_normed_two, axis=0)
    grad_residual = cotangent[0].astype(jnp.float32) + norm_back(
        grad_normed_two, gain_two, scaled_two, inverse_two
    )

    grad_branch = gather_tokens(grad_residual.astype(jnp.bfloat16), 2).reshape(4 * tokens, D)
    grad_attended = right_product(grad_branch, out_weight).astype(jnp.bfloat16)
    grad_attended, grad_gate_up = after((grad_attended, grad_gate_up), grad_branch)
    forth = jnp.dot(hidden, down, preferred_element_type=jnp.float32)
    forth, _ = quad_scatter(after(forth, grad_attended))
    grad_out = left_product(attended, grad_branch).astype(jnp.bfloat16)
    gate_rows = relative_four(
        [
            jnp.concatenate(
                [grad_gate_up[(4 * x + z) * share : (4 * x + z + 1) * share] for x in (0, 1)],
                axis=0,
            )
            for z in range(4)
        ]
    )
    gate_rows = [gate_rows[0]] + [swap(gate_rows[m], "ctx", m) for m in (1, 2, 3)]
    grad_out = sum_rows(after(grad_out, grad_down))
    grad_projected = jnp.concatenate(
        attention_backward(runs, kept, grad_attended, tables), axis=1
    )
    grad_projected, gate_rows, grad_out = after(
        (grad_projected, gate_rows, grad_out), grad_projected
    )
    gate_rows = by_bit(odd, [add_low(gate_rows[m], gate_rows[m + 2]) for m in (0, 1)])
    kept_x, sent_x = by_bit(
        x_bit,
        [
            jnp.concatenate([part[x * share : (x + 1) * share] for part in gate_rows], axis=0)
            for x in (0, 1)
        ],
    )
    came_x = swap(sent_x, "batch", 2)
    partial = right_product(grad_projected, qkv_weight)
    hidden_out = (residual + forth).astype(jnp.bfloat16)

    grad_down = after(grad_down, grad_projected)
    down_kept, down_sent = by_bit(high, [grad_down[:ff_unit], grad_down[ff_unit:]])
    down_came = swap(down_sent, "ctx", 2)

    def whole_columns(parts, start):
        units = [
            [
                parts[x][parity * share : (parity + 1) * share, start : start + ff_part].reshape(
                    share, 2, 2, 2, ff_unit
                )
                for parity in (0, 1)
            ]
            for x in (0, 1)
        ]
        columns = jnp.stack([jnp.stack(pair, axis=4) for pair in units], axis=2)
        return columns.reshape(share, 32 * ff_unit).astype(jnp.float32)

    grad_qkv = sum_rows(left_product(normed_all, grad_projected).astype(jnp.bfloat16))
    grad_qkv_bias = jnp.sum(grad_projected.astype(jnp.float32), axis=0)
    wide_bias = jnp.where(
        jnp.arange(4)[None, None, :, None] == place,
        grad_qkv_bias.reshape(3, members, 1, HEAD_DIM),
        0.0,
    )
    vectors = [
        jnp.sum(partial * scaled_all, axis=0),
        jnp.sum(partial, axis=0),
        grad_gain_two,
        grad_bias_two,
        wide_bias,
    ]
    vectors = jnp.concatenate([part.reshape(32, -1) for part in vectors], axis=1)
    grad_normed_one = scatter_tokens(partial, 1)
    summed = scatter_small(vectors)
    parts = by_bit(x_bit, [kept_x, came_x])
    gate_shard, up_shard = whole_columns(parts, 0), whole_columns(parts, ff_part)
    down_shard = down_kept.astype(jnp.float32) + down_came.astype(jnp.float32)
    grad_tokens = grad_residual + norm_back(grad_normed_one, gain_one, scaled_one, inverse_one)
    out_shard = grad_out.astype(jnp.float32)
    qkv_shard = join_columns(exchange_back(grad_qkv), HEAD_DIM)
    return (
        hidden_out[None],
        grad_tokens[None],
        summed[:share],
        summed[share : 2 * share],
        qkv_shard,
        summed[4 * share :],
        out_shard,
        summed[2 * share : 3 * share],
        summed[3 * share : 4 * share],
        gate_shard,
        up_shard,
        down_shard,
    )


def solution(mesh):
    placed = (
        P("batch", "ctx", None),
        P("batch", "ctx"),
        P(("batch", "ctx")),
        P(("batch", "ctx")),
        P(("batch", "ctx"), None),
        P(("batch", "ctx")),
        P(("batch", "ctx"), None),
        P(("batch", "ctx")),
        P(("batch", "ctx")),
        P(("batch", "ctx"), None),
        P(("batch", "ctx"), None),
        P(("batch", "ctx"), None),
        P("batch", "ctx", None),
    )
    chain_of_four = mesh.shape["batch"] == 8 and mesh.shape["ctx"] == 4
    return jax.shard_map(
        body_chain if chain_of_four else body,
        mesh=mesh,
        in_specs=placed,
        out_specs=(
            P("batch", "ctx", None),
            P("batch", "ctx", None),
            P(("batch", "ctx")),
            P(("batch", "ctx")),
            P(("batch", "ctx"), None),
            P(("batch", "ctx")),
            P(("batch", "ctx"), None),
            P(("batch", "ctx")),
            P(("batch", "ctx")),
            P(("batch", "ctx"), None),
            P(("batch", "ctx"), None),
            P(("batch", "ctx"), None),
        ),
        check_vma=False,
    )
```

```python
import jax
import jax.numpy as jnp
from jax import lax
from jax.experimental import pallas as pl
from jax.experimental.pallas import tpu as pltpu
from jax.sharding import PartitionSpec as P

HEADS = 32
HEAD_DIM = 64
ROT = 16
D = 2048


EPSILON = 1e-05
NEGATIVE = -1e30


def rotary_tables(places):
    steps_half = jnp.arange(ROT // 2, dtype=jnp.float32)
    frequency = 10000.0 ** (-2.0 * steps_half / ROT)
    angles = places.astype(jnp.float32)[:, None] * frequency[None, :]
    angles = jnp.concatenate([angles, angles], axis=1)
    row_count = places.shape[0]
    cosine = jnp.concatenate(
        [jnp.cos(angles), jnp.ones((row_count, HEAD_DIM - ROT), jnp.float32)], axis=1
    )
    sine_table = jnp.concatenate(
        [jnp.sin(angles), jnp.zeros((row_count, HEAD_DIM - ROT), jnp.float32)], axis=1
    )
    return (cosine[:, None, :], sine_table[:, None, :])


def rotate_half(values):
    first_part = values[..., : ROT // 2]
    second_part = values[..., ROT // 2 : ROT]
    return jnp.concatenate([-second_part, first_part, jnp.zeros_like(values[..., ROT:])], axis=-1)


def apply_rotary(values, cosine, sine_table):
    return values * cosine + rotate_half(values) * sine_table


def rotary_back(gradient, cosine, sine_table):
    return gradient * cosine - rotate_half(gradient * sine_table)


def norm_forward(tokens_in):
    centred = tokens_in - jnp.mean(tokens_in, axis=-1, keepdims=True)
    spread = jnp.mean(centred * centred, axis=-1, keepdims=True)
    inverse = lax.rsqrt(spread + EPSILON)
    return (centred * inverse, inverse)


def norm_back(gradient, gain, scaled, inverse):
    weighted = gradient * gain
    return inverse * (
        weighted
        - jnp.mean(weighted, axis=-1, keepdims=True)
        - scaled * jnp.mean(weighted * scaled, axis=-1, keepdims=True)
    )


def left_product(left_side, right_side):
    return lax.dot_general(
        left_side, right_side, (((0,), (0,)), ((), ())), preferred_element_type=jnp.float32
    )


def right_product(left_side, right_side):
    return lax.dot_general(
        left_side, right_side, (((1,), (1,)), ((), ())), preferred_element_type=jnp.float32
    )


def body(
    hidden_in,
    positions,
    norm1_gain,
    norm1_bias,
    w_qkv,
    b_qkv,
    w_out,
    norm2_gain,
    norm2_bias,
    w_gate,
    w_up,
    w_down,
    cotangent,
):
    attn_set = (
        lax.all_gather(norm1_gain, ("batch", "ctx"), axis=0, tiled=True),
        lax.all_gather(norm1_bias, ("batch", "ctx"), axis=0, tiled=True),
        lax.all_gather(w_qkv, ("batch", "ctx"), axis=0, tiled=True),
        lax.all_gather(b_qkv, ("batch", "ctx"), axis=0, tiled=True),
        lax.all_gather(w_out, ("batch", "ctx"), axis=0, tiled=True),
    )
    key_places = lax.all_gather(positions[0], "ctx", axis=0, tiled=True)
    query_places = positions[0]
    tokens_in = hidden_in[0].astype(jnp.float32)
    token_count = tokens_in.shape[0]
    gain_one = attn_set[0].astype(jnp.float32)
    scaled_one, inverse_one = norm_forward(tokens_in)
    normed_one = (scaled_one * gain_one + attn_set[1].astype(jnp.float32)).astype(jnp.bfloat16)
    projected = jnp.dot(normed_one, attn_set[2], preferred_element_type=jnp.float32) + attn_set[
        3
    ].astype(jnp.float32)
    cosine, sine_table = rotary_tables(query_places)
    shaped = projected.reshape(token_count, 3, HEADS, HEAD_DIM)
    queries = apply_rotary(shaped[:, 0], cosine, sine_table).astype(jnp.bfloat16)
    key_local = (
        apply_rotary(shaped[:, 1], cosine, sine_table).astype(jnp.bfloat16).reshape(token_count, D)
    )
    value_local = shaped[:, 2].astype(jnp.bfloat16).reshape(token_count, D)

    def piece_scores(key_piece):
        piece_rows = key_piece.shape[0]
        scores = (
            jnp.einsum(
                "qhd,khd->hqk",
                queries,
                key_piece.reshape(piece_rows, HEADS, HEAD_DIM),
                preferred_element_type=jnp.float32,
            )
            * 0.125
        )
        visible = (key_places[None, :] <= query_places[:, None])[None]
        return (jnp.where(visible, scores, NEGATIVE), visible)

    run_max = jnp.full((HEADS, token_count), NEGATIVE, jnp.float32)
    key_piece = lax.all_gather(key_local, "ctx", axis=0, tiled=True)
    value_piece = lax.all_gather(value_local, "ctx", axis=0, tiled=True)
    piece_rows = key_piece.shape[0]
    scores, visible = piece_scores(key_piece)
    new_max = jnp.maximum(run_max, jnp.max(scores, axis=-1))
    weights = jnp.where(visible, jnp.exp(scores - new_max[..., None]), 0.0)
    run_total = jnp.sum(weights, axis=-1)
    update = jnp.einsum(
        "hqk,khd->qhd",
        weights.astype(jnp.bfloat16),
        value_piece.reshape(piece_rows, HEADS, HEAD_DIM),
        preferred_element_type=jnp.float32,
    )
    accumulated = update
    run_max, run_total, accumulated = (new_max, run_total, accumulated)
    attended_full = accumulated / jnp.transpose(run_total)[..., None]
    log_total = run_max + jnp.log(run_total)
    attended_low = attended_full.reshape(token_count, D).astype(jnp.bfloat16)
    branch = jnp.dot(attended_low, attn_set[4], preferred_element_type=jnp.float32)
    residual = tokens_in + branch
    mlp_set = (
        lax.all_gather(norm2_gain, ("batch", "ctx"), axis=0, tiled=True),
        lax.all_gather(norm2_bias, ("batch", "ctx"), axis=0, tiled=True),
        lax.all_gather(w_gate, ("batch", "ctx"), axis=0, tiled=True),
        lax.all_gather(w_up, ("batch", "ctx"), axis=0, tiled=True),
        lax.all_gather(w_down, ("batch", "ctx"), axis=0, tiled=True),
    )
    scaled_two, inverse_two = norm_forward(residual)
    normed_two = (
        scaled_two * mlp_set[0].astype(jnp.float32) + mlp_set[1].astype(jnp.float32)
    ).astype(jnp.bfloat16)
    gate_value = jnp.dot(normed_two, mlp_set[2], preferred_element_type=jnp.float32)
    up_value = jnp.dot(normed_two, mlp_set[3], preferred_element_type=jnp.float32)
    sigmoid_gate = jax.nn.sigmoid(gate_value)
    activated = gate_value * sigmoid_gate
    hidden = (activated * up_value).astype(jnp.bfloat16)
    hidden_out = (
        residual + jnp.dot(hidden, mlp_set[4], preferred_element_type=jnp.float32)
    ).astype(jnp.bfloat16)
    mlp_back = (
        lax.all_gather(norm2_gain, ("batch", "ctx"), axis=0, tiled=True),
        lax.all_gather(norm2_bias, ("batch", "ctx"), axis=0, tiled=True),
        lax.all_gather(w_gate, ("batch", "ctx"), axis=0, tiled=True),
        lax.all_gather(w_up, ("batch", "ctx"), axis=0, tiled=True),
        lax.all_gather(w_down, ("batch", "ctx"), axis=0, tiled=True),
    )
    grad_output = cotangent[0].astype(jnp.float32)
    grad_mlp = grad_output.astype(jnp.bfloat16)
    grad_down = left_product(hidden, grad_mlp)
    grad_units = right_product(grad_mlp, mlp_back[4])
    grad_gate = (
        grad_units * up_value * sigmoid_gate * (1.0 + gate_value * (1.0 - sigmoid_gate))
    ).astype(jnp.bfloat16)
    grad_up = (grad_units * activated).astype(jnp.bfloat16)
    grad_gate_weight = left_product(normed_two, grad_gate)
    grad_up_weight = left_product(normed_two, grad_up)
    grad_normed_two = right_product(grad_gate, mlp_back[2]) + right_product(grad_up, mlp_back[3])
    grad_gain_two = jnp.sum(grad_normed_two * scaled_two, axis=0)
    grad_bias_two = jnp.sum(grad_normed_two, axis=0)
    grad_residual = grad_output + norm_back(
        grad_normed_two, mlp_back[0].astype(jnp.float32), scaled_two, inverse_two
    )
    mlp_shards = (
        lax.psum_scatter(grad_gain_two, ("batch", "ctx"), scatter_dimension=0, tiled=True),
        lax.psum_scatter(grad_bias_two, ("batch", "ctx"), scatter_dimension=0, tiled=True),
        lax.psum_scatter(grad_gate_weight, ("batch", "ctx"), scatter_dimension=0, tiled=True),
        lax.psum_scatter(grad_up_weight, ("batch", "ctx"), scatter_dimension=0, tiled=True),
        lax.psum_scatter(grad_down, ("batch", "ctx"), scatter_dimension=0, tiled=True),
    )
    attn_back = (
        lax.all_gather(norm1_gain, ("batch", "ctx"), axis=0, tiled=True),
        lax.all_gather(norm1_bias, ("batch", "ctx"), axis=0, tiled=True),
        lax.all_gather(w_qkv, ("batch", "ctx"), axis=0, tiled=True),
        lax.all_gather(b_qkv, ("batch", "ctx"), axis=0, tiled=True),
        lax.all_gather(w_out, ("batch", "ctx"), axis=0, tiled=True),
    )
    grad_branch = grad_residual.astype(jnp.bfloat16)
    grad_out_weight = left_product(attended_low, grad_branch)
    grad_attended = (
        right_product(grad_branch, attn_back[4])
        .astype(jnp.bfloat16)
        .reshape(token_count, HEADS, HEAD_DIM)
    )
    row_dot = jnp.transpose(jnp.sum(grad_attended.astype(jnp.float32) * attended_full, axis=-1))
    key_piece = lax.all_gather(key_local, "ctx", axis=0, tiled=True)
    value_piece = lax.all_gather(value_local, "ctx", axis=0, tiled=True)
    piece_rows = key_piece.shape[0]
    scores, visible = piece_scores(key_piece)
    probabilities = jnp.where(visible, jnp.exp(scores - log_total[..., None]), 0.0)
    value_shaped = value_piece.reshape(piece_rows, HEADS, HEAD_DIM)
    key_shaped = key_piece.reshape(piece_rows, HEADS, HEAD_DIM)
    grad_values = jnp.einsum(
        "hqk,qhd->khd",
        probabilities.astype(jnp.bfloat16),
        grad_attended,
        preferred_element_type=jnp.float32,
    )
    grad_probs = jnp.einsum(
        "qhd,khd->hqk", grad_attended, value_shaped, preferred_element_type=jnp.float32
    )
    grad_scores = (probabilities * (grad_probs - row_dot[..., None])).astype(jnp.bfloat16)
    query_grad = 0.125 * jnp.einsum(
        "hqk,khd->qhd", grad_scores, key_shaped, preferred_element_type=jnp.float32
    )
    grad_keys = 0.125 * jnp.einsum(
        "hqk,qhd->khd", grad_scores, queries, preferred_element_type=jnp.float32
    )
    piece_grad = jnp.concatenate(
        [grad_keys.reshape(piece_rows, D), grad_values.reshape(piece_rows, D)], axis=1
    )
    pair_grad = piece_grad
    query_grad, pair_grad = (query_grad, pair_grad)
    pair_local = lax.psum_scatter(
        pair_grad.astype(jnp.bfloat16), "ctx", scatter_dimension=0, tiled=True
    ).astype(jnp.float32)
    grad_query_lin = rotary_back(query_grad, cosine, sine_table)
    grad_key_lin = rotary_back(
        pair_local[:, :D].reshape(token_count, HEADS, HEAD_DIM), cosine, sine_table
    )
    grad_value_lin = pair_local[:, D:].reshape(token_count, HEADS, HEAD_DIM)
    grad_projected = (
        jnp.stack([grad_query_lin, grad_key_lin, grad_value_lin], axis=1)
        .reshape(token_count, 3 * D)
        .astype(jnp.bfloat16)
    )
    grad_qkv_weight = left_product(normed_one, grad_projected)
    grad_qkv_bias = jnp.sum(grad_projected.astype(jnp.float32), axis=0)
    grad_normed_one = right_product(grad_projected, attn_back[2])
    grad_gain_one = jnp.sum(grad_normed_one * scaled_one, axis=0)
    grad_bias_one = jnp.sum(grad_normed_one, axis=0)
    grad_tokens = grad_residual + norm_back(
        grad_normed_one, attn_back[0].astype(jnp.float32), scaled_one, inverse_one
    )
    attn_shards = (
        lax.psum_scatter(grad_gain_one, ("batch", "ctx"), scatter_dimension=0, tiled=True),
        lax.psum_scatter(grad_bias_one, ("batch", "ctx"), scatter_dimension=0, tiled=True),
        lax.psum_scatter(grad_qkv_weight, ("batch", "ctx"), scatter_dimension=0, tiled=True),
        lax.psum_scatter(grad_qkv_bias, ("batch", "ctx"), scatter_dimension=0, tiled=True),
        lax.psum_scatter(grad_out_weight, ("batch", "ctx"), scatter_dimension=0, tiled=True),
    )
    return (
        hidden_out[None],
        grad_tokens[None],
        attn_shards[0],
        attn_shards[1],
        attn_shards[2],
        attn_shards[3],
        attn_shards[4],
        mlp_shards[0],
        mlp_shards[1],
        mlp_shards[2],
        mlp_shards[3],
        mlp_shards[4],
    )

RUN = 128
PAIR = 2 * HEAD_DIM
VMEM_LIMIT = 48 * 1024 * 1024


def turn(values, tables):
    cosine, sine_up, sine_down = tables
    return (
        values * cosine
        + pltpu.roll(values, ROT // 2, 1) * sine_up
        + pltpu.roll(values, PAIR - ROT // 2, 1) * sine_down
    )


def turn_back(values, tables):
    cosine, sine_up, sine_down = tables
    return (
        values * cosine
        - pltpu.roll(values, ROT // 2, 1) * sine_up
        - pltpu.roll(values, PAIR - ROT // 2, 1) * sine_down
    )


def run_rows(runs, index):
    return pl.ds(pl.multiple_of(runs[index] * RUN, RUN), RUN)


def score_block(query, keys, start):
    scores = lax.dot_general(
        query, keys, (((1,), (1,)), ((), ())), preferred_element_type=jnp.float32
    )
    row = lax.broadcasted_iota(jnp.int32, scores.shape, 0) + start
    column = lax.broadcasted_iota(jnp.int32, scores.shape, 1)
    scores = jnp.where(column <= row, scores, NEGATIVE)
    weights = jnp.exp(scores - jnp.max(scores, axis=1, keepdims=True))
    return weights, jnp.sum(weights, axis=1, keepdims=True)


def head_lanes(values, head):
    lane = lax.broadcasted_iota(jnp.int32, values.shape, 1)
    return jnp.where((lane < HEAD_DIM) == (head == 0), values, jnp.zeros_like(values))


def attention_kernel(runs, q, k, v, cosine, sine_up, sine_down, out, q_kept, k_kept, v_kept):
    length = q.shape[0]
    for index in range(length // RUN):
        rows = run_rows(runs, index)
        place = slice(index * RUN, (index + 1) * RUN)
        tables = cosine[rows, :], sine_up[rows, :], sine_down[rows, :]
        q_kept[place, :] = turn(q[rows, :], tables).astype(jnp.bfloat16)
        k_kept[place, :] = turn(k[rows, :], tables).astype(jnp.bfloat16)
        v_kept[place, :] = v[rows, :].astype(jnp.bfloat16)
    step = 2 * RUN
    for index in range(length // step):
        seen = (index + 1) * step
        query = q_kept[index * step : seen, :]
        result = 0.0
        for head in (0, 1):
            weights, total = score_block(
                head_lanes(query, head) * 0.125, k_kept[:seen, :], index * step
            )
            summed = jnp.dot(
                weights.astype(jnp.bfloat16), v_kept[:seen, :], preferred_element_type=jnp.float32
            )
            result = result + head_lanes(summed / total, head)
        result = result.astype(jnp.bfloat16)
        out[run_rows(runs, 2 * index), :] = result[:RUN]
        out[run_rows(runs, 2 * index + 1), :] = result[RUN:]


def attention_back_kernel(
    runs, q, k, v, grad, cosine, sine_up, sine_down, q_out, k_out, v_out, k_sum, v_sum
):
    length = q.shape[0]
    step = 2 * RUN
    k_sum[...] = jnp.zeros_like(k_sum)
    v_sum[...] = jnp.zeros_like(v_sum)
    for index in range(length // step):
        seen = (index + 1) * step
        query = q[index * step : seen, :]
        pair = [run_rows(runs, 2 * index), run_rows(runs, 2 * index + 1)]
        grad_rows = jnp.concatenate([grad[rows, :] for rows in pair], axis=0)
        grad_query = 0.0
        for head in (0, 1):
            query_head = head_lanes(query, head) * 0.125
            grad_head = head_lanes(grad_rows, head)
            weights, total = score_block(query_head, k[:seen, :], index * step)
            weights = weights / total
            grad_weights = lax.dot_general(
                grad_head, v[:seen, :], (((1,), (1,)), ((), ())), preferred_element_type=jnp.float32
            )
            row_dot = jnp.sum(weights * grad_weights, axis=1, keepdims=True)
            grad_scores = (weights * (grad_weights - row_dot)).astype(jnp.bfloat16)
            grad_query = grad_query + head_lanes(
                jnp.dot(grad_scores, k[:seen, :], preferred_element_type=jnp.float32), head
            )
            k_sum[:seen, :] += left_product(grad_scores, query_head)
            v_sum[:seen, :] += left_product(weights.astype(jnp.bfloat16), grad_head)
        grad_query = grad_query * 0.125
        for part, rows in enumerate(pair):
            tables = cosine[rows, :], sine_up[rows, :], sine_down[rows, :]
            q_out[rows, :] = turn_back(
                grad_query[part * RUN : (part + 1) * RUN], tables
            ).astype(jnp.bfloat16)
    for index in range(length // RUN):
        rows = run_rows(runs, index)
        place = slice(index * RUN, (index + 1) * RUN)
        tables = cosine[rows, :], sine_up[rows, :], sine_down[rows, :]
        k_out[rows, :] = turn_back(k_sum[place, :], tables).astype(jnp.bfloat16)
        v_out[rows, :] = v_sum[place, :].astype(jnp.bfloat16)


def attention_forward(runs, projected, tables, width):
    length = projected.shape[0]
    pairs = width // PAIR
    column = lambda start: pl.BlockSpec((length, PAIR), lambda i, _: (0, i + start))
    whole = pl.BlockSpec((length, PAIR), lambda i, _: (0, 0))
    shape = jax.ShapeDtypeStruct((length, width), jnp.bfloat16)
    return pl.pallas_call(
        attention_kernel,
        out_shape=[shape] * 4,
        grid_spec=pltpu.PrefetchScalarGridSpec(
            num_scalar_prefetch=1,
            grid=(pairs,),
            in_specs=[column(0), column(pairs), column(2 * pairs)] + [whole] * 3,
            out_specs=[column(0)] * 4,
        ),
        compiler_params=pltpu.CompilerParams(vmem_limit_bytes=VMEM_LIMIT),
        cost_estimate=pl.CostEstimate(
            flops=6 * length * length * width,
            bytes_accessed=20 * length * width,
            transcendentals=2 * pairs * length * length,
        ),
        name="attention_forward",
    )(runs, projected, projected, projected, *tables)


def attention_backward(runs, kept, grad, tables):
    length, width = grad.shape
    column = pl.BlockSpec((length, PAIR), lambda i, _: (0, i))
    whole = pl.BlockSpec((length, PAIR), lambda i, _: (0, 0))
    shape = jax.ShapeDtypeStruct((length, width), jnp.bfloat16)
    return pl.pallas_call(
        attention_back_kernel,
        out_shape=[shape] * 3,
        grid_spec=pltpu.PrefetchScalarGridSpec(
            num_scalar_prefetch=1,
            grid=(width // PAIR,),
            in_specs=[column] * 4 + [whole] * 3,
            out_specs=[column] * 3,
            scratch_shapes=[pltpu.VMEM((length, PAIR), jnp.float32)] * 2,
        ),
        compiler_params=pltpu.CompilerParams(vmem_limit_bytes=VMEM_LIMIT),
        cost_estimate=pl.CostEstimate(
            flops=20 * length * length * width,
            bytes_accessed=14 * length * width,
            transcendentals=2 * width // PAIR * length * length,
        ),
        name="attention_backward",
    )(runs, *kept, grad, *tables)


def unit_moves(unit):
    moves = []
    for y in (0, 1):
        for x in (0, 1):
            for r in (0, 1):
                for q in (0, 1):
                    for parity in (0, 1):
                        whole = ((((y * 2 + x) * 2 + r) * 2 + q) * 2 + parity) * unit
                        moves.append((x, parity, whole, ((y * 2 + r) * 2 + q) * unit))
    return moves


def split_kernel(gate, up, out, wide, packed):
    rows, columns = gate.shape
    unit = columns // 32
    for half, weight in enumerate((gate, up)):
        wide[...] = weight[...].astype(jnp.float32)
        for x, parity, whole, place in unit_moves(unit):
            at = half * (columns // 4) + place
            packed[x, parity * rows : (parity + 1) * rows, at : at + unit] = wide[
                :, whole : whole + unit
            ]
    out[...] = packed[...].astype(jnp.bfloat16)


def join_kernel(first, second, gate, up, wide):
    rows, columns = gate.shape
    unit = columns // 32
    for x, part in enumerate((first, second)):
        wide[x] = part[...].astype(jnp.float32)
    for half, weight in enumerate((gate, up)):
        for x, parity, whole, place in unit_moves(unit):
            at = half * (columns // 4) + place
            weight[:, whole : whole + unit] = wide[
                x, parity * rows : (parity + 1) * rows, at : at + unit
            ]


def split_units(gate, up):
    rows, columns = gate.shape
    packed = (2, 2 * rows, columns // 2)
    return pl.pallas_call(
        split_kernel,
        out_shape=jax.ShapeDtypeStruct(packed, jnp.bfloat16),
        scratch_shapes=[
            pltpu.VMEM((rows, columns), jnp.float32),
            pltpu.VMEM(packed, jnp.float32),
        ],
        compiler_params=pltpu.CompilerParams(vmem_limit_bytes=VMEM_LIMIT),
        name="split_units",
    )(gate, up)


def join_units(first, second):
    rows, columns = first.shape[0] // 2, 2 * first.shape[1]
    shape = jax.ShapeDtypeStruct((rows, columns), jnp.float32)
    return pl.pallas_call(
        join_kernel,
        out_shape=[shape, shape],
        scratch_shapes=[pltpu.VMEM((2, *first.shape), jnp.float32)],
        compiler_params=pltpu.CompilerParams(vmem_limit_bytes=VMEM_LIMIT),
        name="join_units",
    )(first, second)


def pair_tables(places):
    cosine, sine_table = rotary_tables(places)
    cosine, sine_table = cosine[:, 0], sine_table[:, 0]
    first = jnp.arange(HEAD_DIM) < ROT // 2
    up = jnp.where(first, 0.0, sine_table)
    down = jnp.where(first, -sine_table, 0.0)
    return [jnp.concatenate([table, table], axis=1) for table in (cosine, up, down)]


def swap(values, axis, mask):
    return lax.ppermute(values, axis, [(i, i ^ mask) for i in range(lax.axis_size(axis))])


def add_low(left, right):
    return (left.astype(jnp.float32) + right.astype(jnp.float32)).astype(jnp.bfloat16)


def relative_four(parts):
    place = lax.axis_index("ctx")
    odd, high = place % 2 == 1, place // 2 == 1
    once = [jnp.where(odd, parts[j ^ 1], parts[j]) for j in range(4)]
    return [jnp.where(high, once[j ^ 2], once[j]) for j in range(4)]


def after(values, *earlier):
    return lax.optimization_barrier((values, earlier))[0]


def greet(place, last):
    barrier = pltpu.get_barrier_semaphore()
    for there, near in ((place > 0, place - 1), (place < last, place + 1)):

        @pl.when(there)
        def _():
            pl.semaphore_signal(
                barrier, inc=1, device_id={"ctx": near}, device_id_type=pl.DeviceIdType.MESH
            )

    peers = jnp.where(place > 0, 1, 0) + jnp.where(place < last, 1, 0)
    pl.semaphore_wait(barrier, peers)


def towards(source, target, send, receive, device):
    return pltpu.make_async_remote_copy(
        src_ref=source,
        dst_ref=target,
        send_sem=send,
        recv_sem=receive,
        device_id={"ctx": device},
        device_id_type=pl.DeviceIdType.MESH,
    )


def gather_kernel(own, out, local, send_up, receive_up, send_down, receive_down):
    place = lax.axis_index("ctx")
    last = out.shape[0] - 1
    greet(place, last)
    mine = pltpu.make_async_copy(own, out.at[place], local)
    mine.start()
    for step in range(last):
        up_from = jnp.maximum(place - step, 0)
        down_from = jnp.minimum(place + step, last)
        source_up = own if step == 0 else out.at[up_from]
        source_down = own if step == 0 else out.at[down_from]
        up = towards(
            source_up,
            out.at[up_from],
            send_up.at[step],
            receive_up.at[step],
            jnp.minimum(place + 1, last),
        )
        down = towards(
            source_down,
            out.at[down_from],
            send_down.at[step],
            receive_down.at[step],
            jnp.maximum(place - 1, 0),
        )

        @pl.when((place >= step) & (place < last))
        def _():
            up.start()

        @pl.when((place <= last - step) & (place > 0))
        def _():
            down.start()

        @pl.when(place >= step + 1)
        def _():
            up.wait_recv()

        @pl.when(place <= last - step - 1)
        def _():
            down.wait_recv()

        @pl.when((place >= step) & (place < last))
        def _():
            up.wait_send()

        @pl.when((place <= last - step) & (place > 0))
        def _():
            down.wait_send()

    mine.wait()


def gather_tokens(block, group):
    size = lax.axis_size("ctx")
    return pl.pallas_call(
        gather_kernel,
        out_shape=jax.ShapeDtypeStruct((size, *block.shape), block.dtype),
        in_specs=[pl.BlockSpec(memory_space=pl.ANY)],
        out_specs=pl.BlockSpec(memory_space=pl.ANY),
        scratch_shapes=[pltpu.SemaphoreType.DMA] + [pltpu.SemaphoreType.DMA((size - 1,))] * 4,
        compiler_params=pltpu.CompilerParams(collective_id=group, has_side_effects=True),
        cost_estimate=pl.CostEstimate(
            flops=0, bytes_accessed=500 * block.size, transcendentals=0
        ),
        name="gather_tokens",
    )(block)


def scatter_kernel(
    partial, out, sum_up, sum_down, in_up, in_down, send_up, receive_up, send_down, receive_down
):
    place = lax.axis_index("ctx")
    last = partial.shape[0] - 1
    greet(place, last)
    for step in range(last):
        up_to = jnp.minimum(place + last - step, last)
        down_to = jnp.maximum(place - last + step, 0)
        goes_up = (place <= step) & (place < last)
        goes_down = (place >= last - step) & (place > 0)

        @pl.when(goes_up)
        def _():
            sum_up[step] = partial[up_to]

        @pl.when(goes_down)
        def _():
            sum_down[step] = partial[down_to]

        if step > 0:

            @pl.when(goes_up & (place > 0))
            def _():
                sum_up[step] = add_low(sum_up[step], in_up[step - 1])

            @pl.when(goes_down & (place < last))
            def _():
                sum_down[step] = add_low(sum_down[step], in_down[step - 1])

        up = towards(
            sum_up.at[step],
            in_up.at[step],
            send_up.at[step],
            receive_up.at[step],
            jnp.minimum(place + 1, last),
        )
        down = towards(
            sum_down.at[step],
            in_down.at[step],
            send_down.at[step],
            receive_down.at[step],
            jnp.maximum(place - 1, 0),
        )

        @pl.when(goes_up)
        def _():
            up.start()

        @pl.when(goes_down)
        def _():
            down.start()

        if step == 0:
            out[...] = partial[place].astype(jnp.float32)

        @pl.when((place > 0) & (place - 1 <= step))
        def _():
            up.wait_recv()

        @pl.when((place < last) & (place + 1 >= last - step))
        def _():
            down.wait_recv()

        @pl.when(goes_up)
        def _():
            up.wait_send()

        @pl.when(goes_down)
        def _():
            down.wait_send()

    @pl.when(place > 0)
    def _():
        out[...] += in_up[last - 1].astype(jnp.float32)

    @pl.when(place < last)
    def _():
        out[...] += in_down[last - 1].astype(jnp.float32)


def scatter_tokens(partial, group):
    size = lax.axis_size("ctx")
    partial = partial.astype(jnp.bfloat16).reshape(size, -1, partial.shape[1])
    block = partial.shape[1:]
    buffer = pltpu.VMEM((size - 1, *block), jnp.bfloat16)
    return pl.pallas_call(
        scatter_kernel,
        out_shape=jax.ShapeDtypeStruct(block, jnp.float32),
        in_specs=[pl.BlockSpec(memory_space=pltpu.VMEM)],
        out_specs=pl.BlockSpec(memory_space=pltpu.VMEM),
        scratch_shapes=[buffer] * 4 + [pltpu.SemaphoreType.DMA((size - 1,))] * 4,
        compiler_params=pltpu.CompilerParams(
            collective_id=group, has_side_effects=True, vmem_limit_bytes=VMEM_LIMIT
        ),
        cost_estimate=pl.CostEstimate(
            flops=0, bytes_accessed=150 * partial.size, transcendentals=0
        ),
        name="scatter_tokens",
    )(partial)


def gather_small(values):
    every = values[None]
    for mask in (1, 2, 4):
        every = jnp.concatenate([every, swap(every, "batch", mask)], axis=0)
    return every


def scatter_small(vectors):
    own, place = lax.axis_index("batch"), lax.axis_index("ctx")
    index = jnp.arange(32)
    rest = jnp.take(vectors, ((index % 8) ^ own) * 4 + ((index // 8) ^ place), axis=0)
    for axis, mask in (("ctx", 2), ("ctx", 1), ("batch", 4), ("batch", 2), ("batch", 1)):
        middle = rest.shape[0] // 2
        rest = rest[:middle] + swap(rest[middle:], axis, mask)
    return rest[0]


def by_bit(bit, parts):
    return jnp.where(bit, parts[1], parts[0]), jnp.where(bit, parts[0], parts[1])


def quad_gather(block, between=None):
    half = block.shape[0] // 2
    from_x = swap(block, "batch", 2)
    from_z = swap(block, "ctx", 1)
    if between is not None:
        from_x, from_z = between((from_x, from_z))
    top = swap(from_z[:half], "batch", 2)
    low = swap(from_x[half:], "ctx", 1)
    return jnp.concatenate([block, from_x, from_z, top, low], axis=0)


def quad_scatter(partial, work=None):
    rows = partial.shape[0] // 4
    half = rows // 2
    low_bits = partial[rows:].astype(jnp.bfloat16)
    x_top, x_low, z_top, z_low, d_top, d_low = [
        low_bits[j * half : (j + 1) * half] for j in range(6)
    ]
    top = swap(jnp.concatenate([z_top, d_top], axis=0), "ctx", 1)
    low = swap(jnp.concatenate([x_low, d_low], axis=0), "batch", 2)
    result = None
    if work is not None:
        result = work()
        top, low = after((top, low), result)
    top_last = swap(add_low(x_top, top[half:]), "batch", 2)
    low_last = swap(add_low(z_low, low[half:]), "ctx", 1)
    first = jnp.concatenate([top[:half], low[:half]], axis=0).astype(jnp.float32)
    last = jnp.concatenate([top_last, low_last], axis=0).astype(jnp.float32)
    return partial[:rows] + first + last, result


def swap_block_order(values):
    size = values.shape[1] // 8
    order = (0, 2, 1, 3, 4, 6, 5, 7)
    return jnp.concatenate([values[:, j * size : (j + 1) * size] for j in order], axis=1)


SAME_X = [[0, 1, 4, 5], [2, 3, 6, 7]]


def split_columns(weight, unit):
    rows, columns = weight.shape
    pieces = weight.reshape(rows, columns // (4 * unit), 4, unit)
    return [pieces[:, :, j].reshape(rows, columns // 4) for j in range(4)]


def join_columns(parts, unit):
    rows, columns = parts[0].shape
    spread = jnp.stack([part.reshape(rows, columns // unit, unit) for part in parts], axis=2)
    return spread.reshape(rows, 4 * columns)


def body_chain(
    hidden_in,
    positions,
    norm1_gain,
    norm1_bias,
    w_qkv,
    b_qkv,
    w_out,
    norm2_gain,
    norm2_bias,
    w_gate,
    w_up,
    w_down,
    cotangent,
):
    place = lax.axis_index("ctx")
    members = HEADS // 4
    width = members * HEAD_DIM
    share = norm1_gain.shape[0]
    ff_unit = w_down.shape[0]
    ff_part = 8 * ff_unit
    tokens = hidden_in.shape[1]

    coarse, fine = jnp.divmod(positions[0], 256)
    small = gather_small(
        jnp.concatenate(
            [norm1_gain, norm1_bias, norm2_gain, norm2_bias, b_qkv]
            + [part.astype(jnp.bfloat16) for part in (coarse, fine)]
        )
    )
    kept_small = small.shape[1]
    extra_rows = -(-small.size // (16 * D)) * 16
    extra = jnp.pad(small.reshape(-1), (0, extra_rows * D - small.size)).reshape(-1, D)
    token_blocks = gather_tokens(jnp.concatenate([hidden_in[0], extra], axis=0), 0)
    arrived_tokens = token_blocks
    small = token_blocks[:, tokens:].reshape(4, -1)[:, : small.size].reshape(4, 8, kept_small)
    tokens_all = token_blocks[:, :tokens].reshape(4 * tokens, D)
    kept = kept_small - 2 * tokens
    places = small[:, 0, kept:].astype(jnp.float32).astype(jnp.int32)
    places = (places[:, :tokens] * 256 + places[:, tokens:]).reshape(-1)
    index = jnp.arange(32)
    index = index % 4 * 8 + ((index // 4) ^ lax.axis_index("batch"))
    small = jnp.take(small.reshape(32, kept_small), index, axis=0)[:, :kept]
    gain_one = small[:, :share].reshape(-1).astype(jnp.float32)
    bias_one = small[:, share : 2 * share].reshape(-1).astype(jnp.float32)
    gain_two = small[:, 2 * share : 3 * share].reshape(-1).astype(jnp.float32)
    bias_two = small[:, 3 * share : 4 * share].reshape(-1).astype(jnp.float32)
    qkv_bias = small[:, 4 * share :].reshape(3, members, 4, HEAD_DIM)
    qkv_bias = lax.dynamic_index_in_dim(qkv_bias, place, 2, keepdims=False)
    qkv_bias = qkv_bias.reshape(3 * width).astype(jnp.float32)

    def exchange(pieces):
        pieces = relative_four(pieces)
        return [pieces[0]] + [swap(pieces[m], "ctx", m) for m in (1, 2, 3)]

    def gather_rows(arrived):
        rows = jnp.concatenate(relative_four(arrived), axis=0)
        return lax.all_gather(rows, "batch", axis=0, tiled=True)

    def sum_rows(gradient):
        return lax.psum_scatter(gradient, "batch", scatter_dimension=0, tiled=True)

    def exchange_back(mine):
        arrived = exchange([mine[j * share : (j + 1) * share] for j in range(4)])
        return [part.astype(jnp.float32) for part in relative_four(arrived)]

    qkv_weight = gather_rows(exchange(split_columns(after(w_qkv, extra), HEAD_DIM)))
    out_weight = lax.all_gather(w_out, "batch", axis=0, tiled=True)

    x_bit = lax.axis_index("batch") // 2 % 2 == 1
    odd, high = place % 2 == 1, place // 2 == 1

    kept_x, sent_x = by_bit(x_bit, split_units(w_gate, w_up))
    came_x = swap(sent_x, "batch", 2)
    first_x, second_x = by_bit(x_bit, [kept_x, came_x])
    for_parity = by_bit(
        odd,
        [
            jnp.concatenate(
                [part[parity * share : (parity + 1) * share] for part in (first_x, second_x)],
                axis=0,
            )
            for parity in (0, 1)
        ],
    )
    for_parity, cot_own = after((for_parity, cotangent[0]), arrived_tokens)
    gate_pieces = [for_parity[0]] + [swap(for_parity[m % 2], "ctx", m) for m in (1, 2, 3)]
    tables = pair_tables(places)
    starts = places[::RUN] // RUN
    order = jnp.arange(starts.shape[0])
    runs = jnp.sum(jnp.where(starts[None, :] == order[:, None], order[None, :], 0), axis=1)
    runs = runs.astype(jnp.int32)
    scaled_all, inverse_all = norm_forward(tokens_all.astype(jnp.float32))
    scaled_one = lax.dynamic_slice_in_dim(scaled_all, place * tokens, tokens, axis=0)
    inverse_one = lax.dynamic_slice_in_dim(inverse_all, place * tokens, tokens, axis=0)
    normed_all = (scaled_all * gain_one + bias_one).astype(jnp.bfloat16)
    projected = jnp.dot(normed_all, qkv_weight, preferred_element_type=jnp.float32) + qkv_bias
    attended, *kept = attention_forward(runs, projected, tables, width)
    branch = scatter_tokens(jnp.dot(attended, out_weight, preferred_element_type=jnp.float32), 1)
    gate_pieces = after(gate_pieces, attended)
    down_piece = after(swap(after(w_down, gate_pieces), "ctx", 2), branch)
    cot_quad = quad_gather(cot_own, lambda passed: after(passed, attended))
    gate_pieces = relative_four(gate_pieces)
    gate_up = lax.all_gather(
        jnp.concatenate(
            [
                gate_pieces[z][x * share : (x + 1) * share]
                for x in (0, 1)
                for z in range(4)
            ],
            axis=0,
        ),
        "batch",
        axis=0,
        tiled=True,
        axis_index_groups=SAME_X,
    )
    down = lax.all_gather(
        jnp.concatenate(by_bit(high, [w_down, down_piece]), axis=0),
        "batch",
        axis=0,
        tiled=True,
        axis_index_groups=SAME_X,
    )

    residual = hidden_in[0].astype(jnp.float32) + branch

    scaled_two, inverse_two = norm_forward(residual)
    normed_quad = quad_gather(
        swap_block_order((scaled_two * gain_two + bias_two).astype(jnp.bfloat16))
    )
    both = jnp.dot(normed_quad, gate_up, preferred_element_type=jnp.float32)
    gate_value, up_value = both[:, :ff_part], both[:, ff_part:]
    sigmoid_gate = jax.nn.sigmoid(gate_value)
    activated = gate_value * sigmoid_gate
    hidden = (activated * up_value).astype(jnp.bfloat16)
    grad_units = right_product(cot_quad, down)
    grad_gate = grad_units * up_value * sigmoid_gate * (1.0 + gate_value * (1.0 - sigmoid_gate))
    grad_both = jnp.concatenate([grad_gate, grad_units * activated], axis=1).astype(jnp.bfloat16)
    grad_normed_two, grad_gate_up = quad_scatter(
        right_product(grad_both, gate_up),
        lambda: (
            left_product(hidden, cot_quad).astype(jnp.bfloat16),
            left_product(normed_quad, grad_both).astype(jnp.bfloat16),
        ),
    )
    grad_down, grad_gate_up = grad_gate_up
    grad_normed_two = swap_block_order(grad_normed_two)

    def sum_quarter(gradient):
        return lax.psum_scatter(
            gradient, "batch", scatter_dimension=0, tiled=True, axis_index_groups=SAME_X
        )

    grad_down = sum_quarter(grad_down)
    grad_gate_up = sum_quarter(grad_gate_up)
    grad_gain_two = jnp.sum(grad_normed_two * scaled_two, axis=0)
    grad_bias_two = jnp.sum(grad_normed_two, axis=0)
    grad_residual = cotangent[0].astype(jnp.float32) + norm_back(
        grad_normed_two, gain_two, scaled_two, inverse_two
    )

    grad_branch = gather_tokens(grad_residual.astype(jnp.bfloat16), 2).reshape(4 * tokens, D)
    grad_attended = right_product(grad_branch, out_weight).astype(jnp.bfloat16)
    grad_attended, grad_gate_up = after((grad_attended, grad_gate_up), grad_branch)
    forth = jnp.dot(hidden, down, preferred_element_type=jnp.float32)
    forth, _ = quad_scatter(after(forth, grad_attended))
    grad_out = left_product(attended, grad_branch).astype(jnp.bfloat16)
    gate_rows = relative_four(
        [
            jnp.concatenate(
                [grad_gate_up[(4 * x + z) * share : (4 * x + z + 1) * share] for x in (0, 1)],
                axis=0,
            )
            for z in range(4)
        ]
    )
    gate_rows = [gate_rows[0]] + [swap(gate_rows[m], "ctx", m) for m in (1, 2, 3)]
    grad_out = sum_rows(after(grad_out, grad_down))
    grad_projected = jnp.concatenate(
        attention_backward(runs, kept, grad_attended, tables), axis=1
    )
    grad_projected, gate_rows, grad_out = after(
        (grad_projected, gate_rows, grad_out), grad_projected
    )
    gate_rows = by_bit(odd, [add_low(gate_rows[m], gate_rows[m + 2]) for m in (0, 1)])
    kept_x, sent_x = by_bit(
        x_bit,
        [
            jnp.concatenate([part[x * share : (x + 1) * share] for part in gate_rows], axis=0)
            for x in (0, 1)
        ],
    )
    came_x = swap(sent_x, "batch", 2)
    partial = right_product(grad_projected, qkv_weight)
    hidden_out = (residual + forth).astype(jnp.bfloat16)

    grad_down = after(grad_down, grad_projected)
    down_kept, down_sent = by_bit(high, [grad_down[:ff_unit], grad_down[ff_unit:]])
    down_came = swap(down_sent, "ctx", 2)

    grad_qkv = sum_rows(left_product(normed_all, grad_projected).astype(jnp.bfloat16))
    grad_qkv_bias = jnp.sum(grad_projected.astype(jnp.float32), axis=0)
    wide_bias = jnp.where(
        jnp.arange(4)[None, None, :, None] == place,
        grad_qkv_bias.reshape(3, members, 1, HEAD_DIM),
        0.0,
    )
    vectors = [
        jnp.sum(partial * scaled_all, axis=0),
        jnp.sum(partial, axis=0),
        grad_gain_two,
        grad_bias_two,
        wide_bias,
    ]
    vectors = jnp.concatenate([part.reshape(32, -1) for part in vectors], axis=1)
    grad_normed_one = scatter_tokens(partial, 1)
    summed = scatter_small(vectors)
    parts = by_bit(x_bit, [kept_x, came_x])
    gate_shard, up_shard = join_units(*parts)
    down_shard = down_kept.astype(jnp.float32) + down_came.astype(jnp.float32)
    grad_tokens = grad_residual + norm_back(grad_normed_one, gain_one, scaled_one, inverse_one)
    out_shard = grad_out.astype(jnp.float32)
    qkv_shard = join_columns(exchange_back(grad_qkv), HEAD_DIM)
    return (
        hidden_out[None],
        grad_tokens[None],
        summed[:share],
        summed[share : 2 * share],
        qkv_shard,
        summed[4 * share :],
        out_shard,
        summed[2 * share : 3 * share],
        summed[3 * share : 4 * share],
        gate_shard,
        up_shard,
        down_shard,
    )


def solution(mesh):
    placed = (
        P("batch", "ctx", None),
        P("batch", "ctx"),
        P(("batch", "ctx")),
        P(("batch", "ctx")),
        P(("batch", "ctx"), None),
        P(("batch", "ctx")),
        P(("batch", "ctx"), None),
        P(("batch", "ctx")),
        P(("batch", "ctx")),
        P(("batch", "ctx"), None),
        P(("batch", "ctx"), None),
        P(("batch", "ctx"), None),
        P("batch", "ctx", None),
    )
    chain_of_four = mesh.shape["batch"] == 8 and mesh.shape["ctx"] == 4
    return jax.shard_map(
        body_chain if chain_of_four else body,
        mesh=mesh,
        in_specs=placed,
        out_specs=(
            P("batch", "ctx", None),
            P("batch", "ctx", None),
            P(("batch", "ctx")),
            P(("batch", "ctx")),
            P(("batch", "ctx"), None),
            P(("batch", "ctx")),
            P(("batch", "ctx"), None),
            P(("batch", "ctx")),
            P(("batch", "ctx")),
            P(("batch", "ctx"), None),
            P(("batch", "ctx"), None),
            P(("batch", "ctx"), None),
        ),
        check_vma=False,
    )
```

```python
import jax
import jax.numpy as jnp
from jax import lax
from jax.experimental import pallas as pl
from jax.experimental.pallas import tpu as pltpu
from jax.sharding import PartitionSpec as P

HEADS = 32
HEAD_DIM = 64
ROT = 16
D = 2048


EPSILON = 1e-05
NEGATIVE = -1e30


def rotary_tables(places):
    steps_half = jnp.arange(ROT // 2, dtype=jnp.float32)
    frequency = 10000.0 ** (-2.0 * steps_half / ROT)
    angles = places.astype(jnp.float32)[:, None] * frequency[None, :]
    angles = jnp.concatenate([angles, angles], axis=1)
    row_count = places.shape[0]
    cosine = jnp.concatenate(
        [jnp.cos(angles), jnp.ones((row_count, HEAD_DIM - ROT), jnp.float32)], axis=1
    )
    sine_table = jnp.concatenate(
        [jnp.sin(angles), jnp.zeros((row_count, HEAD_DIM - ROT), jnp.float32)], axis=1
    )
    return (cosine[:, None, :], sine_table[:, None, :])


def rotate_half(values):
    first_part = values[..., : ROT // 2]
    second_part = values[..., ROT // 2 : ROT]
    return jnp.concatenate([-second_part, first_part, jnp.zeros_like(values[..., ROT:])], axis=-1)


def apply_rotary(values, cosine, sine_table):
    return values * cosine + rotate_half(values) * sine_table


def rotary_back(gradient, cosine, sine_table):
    return gradient * cosine - rotate_half(gradient * sine_table)


def norm_forward(tokens_in):
    centred = tokens_in - jnp.mean(tokens_in, axis=-1, keepdims=True)
    spread = jnp.mean(centred * centred, axis=-1, keepdims=True)
    inverse = lax.rsqrt(spread + EPSILON)
    return (centred * inverse, inverse)


def norm_back(gradient, gain, scaled, inverse):
    weighted = gradient * gain
    return inverse * (
        weighted
        - jnp.mean(weighted, axis=-1, keepdims=True)
        - scaled * jnp.mean(weighted * scaled, axis=-1, keepdims=True)
    )


def left_product(left_side, right_side):
    return lax.dot_general(
        left_side, right_side, (((0,), (0,)), ((), ())), preferred_element_type=jnp.float32
    )


def right_product(left_side, right_side):
    return lax.dot_general(
        left_side, right_side, (((1,), (1,)), ((), ())), preferred_element_type=jnp.float32
    )


def body(
    hidden_in,
    positions,
    norm1_gain,
    norm1_bias,
    w_qkv,
    b_qkv,
    w_out,
    norm2_gain,
    norm2_bias,
    w_gate,
    w_up,
    w_down,
    cotangent,
):
    attn_set = (
        lax.all_gather(norm1_gain, ("batch", "ctx"), axis=0, tiled=True),
        lax.all_gather(norm1_bias, ("batch", "ctx"), axis=0, tiled=True),
        lax.all_gather(w_qkv, ("batch", "ctx"), axis=0, tiled=True),
        lax.all_gather(b_qkv, ("batch", "ctx"), axis=0, tiled=True),
        lax.all_gather(w_out, ("batch", "ctx"), axis=0, tiled=True),
    )
    key_places = lax.all_gather(positions[0], "ctx", axis=0, tiled=True)
    query_places = positions[0]
    tokens_in = hidden_in[0].astype(jnp.float32)
    token_count = tokens_in.shape[0]
    gain_one = attn_set[0].astype(jnp.float32)
    scaled_one, inverse_one = norm_forward(tokens_in)
    normed_one = (scaled_one * gain_one + attn_set[1].astype(jnp.float32)).astype(jnp.bfloat16)
    projected = jnp.dot(normed_one, attn_set[2], preferred_element_type=jnp.float32) + attn_set[
        3
    ].astype(jnp.float32)
    cosine, sine_table = rotary_tables(query_places)
    shaped = projected.reshape(token_count, 3, HEADS, HEAD_DIM)
    queries = apply_rotary(shaped[:, 0], cosine, sine_table).astype(jnp.bfloat16)
    key_local = (
        apply_rotary(shaped[:, 1], cosine, sine_table).astype(jnp.bfloat16).reshape(token_count, D)
    )
    value_local = shaped[:, 2].astype(jnp.bfloat16).reshape(token_count, D)

    def piece_scores(key_piece):
        piece_rows = key_piece.shape[0]
        scores = (
            jnp.einsum(
                "qhd,khd->hqk",
                queries,
                key_piece.reshape(piece_rows, HEADS, HEAD_DIM),
                preferred_element_type=jnp.float32,
            )
            * 0.125
        )
        visible = (key_places[None, :] <= query_places[:, None])[None]
        return (jnp.where(visible, scores, NEGATIVE), visible)

    run_max = jnp.full((HEADS, token_count), NEGATIVE, jnp.float32)
    key_piece = lax.all_gather(key_local, "ctx", axis=0, tiled=True)
    value_piece = lax.all_gather(value_local, "ctx", axis=0, tiled=True)
    piece_rows = key_piece.shape[0]
    scores, visible = piece_scores(key_piece)
    new_max = jnp.maximum(run_max, jnp.max(scores, axis=-1))
    weights = jnp.where(visible, jnp.exp(scores - new_max[..., None]), 0.0)
    run_total = jnp.sum(weights, axis=-1)
    update = jnp.einsum(
        "hqk,khd->qhd",
        weights.astype(jnp.bfloat16),
        value_piece.reshape(piece_rows, HEADS, HEAD_DIM),
        preferred_element_type=jnp.float32,
    )
    accumulated = update
    run_max, run_total, accumulated = (new_max, run_total, accumulated)
    attended_full = accumulated / jnp.transpose(run_total)[..., None]
    log_total = run_max + jnp.log(run_total)
    attended_low = attended_full.reshape(token_count, D).astype(jnp.bfloat16)
    branch = jnp.dot(attended_low, attn_set[4], preferred_element_type=jnp.float32)
    residual = tokens_in + branch
    mlp_set = (
        lax.all_gather(norm2_gain, ("batch", "ctx"), axis=0, tiled=True),
        lax.all_gather(norm2_bias, ("batch", "ctx"), axis=0, tiled=True),
        lax.all_gather(w_gate, ("batch", "ctx"), axis=0, tiled=True),
        lax.all_gather(w_up, ("batch", "ctx"), axis=0, tiled=True),
        lax.all_gather(w_down, ("batch", "ctx"), axis=0, tiled=True),
    )
    scaled_two, inverse_two = norm_forward(residual)
    normed_two = (
        scaled_two * mlp_set[0].astype(jnp.float32) + mlp_set[1].astype(jnp.float32)
    ).astype(jnp.bfloat16)
    gate_value = jnp.dot(normed_two, mlp_set[2], preferred_element_type=jnp.float32)
    up_value = jnp.dot(normed_two, mlp_set[3], preferred_element_type=jnp.float32)
    sigmoid_gate = jax.nn.sigmoid(gate_value)
    activated = gate_value * sigmoid_gate
    hidden = (activated * up_value).astype(jnp.bfloat16)
    hidden_out = (
        residual + jnp.dot(hidden, mlp_set[4], preferred_element_type=jnp.float32)
    ).astype(jnp.bfloat16)
    mlp_back = (
        lax.all_gather(norm2_gain, ("batch", "ctx"), axis=0, tiled=True),
        lax.all_gather(norm2_bias, ("batch", "ctx"), axis=0, tiled=True),
        lax.all_gather(w_gate, ("batch", "ctx"), axis=0, tiled=True),
        lax.all_gather(w_up, ("batch", "ctx"), axis=0, tiled=True),
        lax.all_gather(w_down, ("batch", "ctx"), axis=0, tiled=True),
    )
    grad_output = cotangent[0].astype(jnp.float32)
    grad_mlp = grad_output.astype(jnp.bfloat16)
    grad_down = left_product(hidden, grad_mlp)
    grad_units = right_product(grad_mlp, mlp_back[4])
    grad_gate = (
        grad_units * up_value * sigmoid_gate * (1.0 + gate_value * (1.0 - sigmoid_gate))
    ).astype(jnp.bfloat16)
    grad_up = (grad_units * activated).astype(jnp.bfloat16)
    grad_gate_weight = left_product(normed_two, grad_gate)
    grad_up_weight = left_product(normed_two, grad_up)
    grad_normed_two = right_product(grad_gate, mlp_back[2]) + right_product(grad_up, mlp_back[3])
    grad_gain_two = jnp.sum(grad_normed_two * scaled_two, axis=0)
    grad_bias_two = jnp.sum(grad_normed_two, axis=0)
    grad_residual = grad_output + norm_back(
        grad_normed_two, mlp_back[0].astype(jnp.float32), scaled_two, inverse_two
    )
    mlp_shards = (
        lax.psum_scatter(grad_gain_two, ("batch", "ctx"), scatter_dimension=0, tiled=True),
        lax.psum_scatter(grad_bias_two, ("batch", "ctx"), scatter_dimension=0, tiled=True),
        lax.psum_scatter(grad_gate_weight, ("batch", "ctx"), scatter_dimension=0, tiled=True),
        lax.psum_scatter(grad_up_weight, ("batch", "ctx"), scatter_dimension=0, tiled=True),
        lax.psum_scatter(grad_down, ("batch", "ctx"), scatter_dimension=0, tiled=True),
    )
    attn_back = (
        lax.all_gather(norm1_gain, ("batch", "ctx"), axis=0, tiled=True),
        lax.all_gather(norm1_bias, ("batch", "ctx"), axis=0, tiled=True),
        lax.all_gather(w_qkv, ("batch", "ctx"), axis=0, tiled=True),
        lax.all_gather(b_qkv, ("batch", "ctx"), axis=0, tiled=True),
        lax.all_gather(w_out, ("batch", "ctx"), axis=0, tiled=True),
    )
    grad_branch = grad_residual.astype(jnp.bfloat16)
    grad_out_weight = left_product(attended_low, grad_branch)
    grad_attended = (
        right_product(grad_branch, attn_back[4])
        .astype(jnp.bfloat16)
        .reshape(token_count, HEADS, HEAD_DIM)
    )
    row_dot = jnp.transpose(jnp.sum(grad_attended.astype(jnp.float32) * attended_full, axis=-1))
    key_piece = lax.all_gather(key_local, "ctx", axis=0, tiled=True)
    value_piece = lax.all_gather(value_local, "ctx", axis=0, tiled=True)
    piece_rows = key_piece.shape[0]
    scores, visible = piece_scores(key_piece)
    probabilities = jnp.where(visible, jnp.exp(scores - log_total[..., None]), 0.0)
    value_shaped = value_piece.reshape(piece_rows, HEADS, HEAD_DIM)
    key_shaped = key_piece.reshape(piece_rows, HEADS, HEAD_DIM)
    grad_values = jnp.einsum(
        "hqk,qhd->khd",
        probabilities.astype(jnp.bfloat16),
        grad_attended,
        preferred_element_type=jnp.float32,
    )
    grad_probs = jnp.einsum(
        "qhd,khd->hqk", grad_attended, value_shaped, preferred_element_type=jnp.float32
    )
    grad_scores = (probabilities * (grad_probs - row_dot[..., None])).astype(jnp.bfloat16)
    query_grad = 0.125 * jnp.einsum(
        "hqk,khd->qhd", grad_scores, key_shaped, preferred_element_type=jnp.float32
    )
    grad_keys = 0.125 * jnp.einsum(
        "hqk,qhd->khd", grad_scores, queries, preferred_element_type=jnp.float32
    )
    piece_grad = jnp.concatenate(
        [grad_keys.reshape(piece_rows, D), grad_values.reshape(piece_rows, D)], axis=1
    )
    pair_grad = piece_grad
    query_grad, pair_grad = (query_grad, pair_grad)
    pair_local = lax.psum_scatter(
        pair_grad.astype(jnp.bfloat16), "ctx", scatter_dimension=0, tiled=True
    ).astype(jnp.float32)
    grad_query_lin = rotary_back(query_grad, cosine, sine_table)
    grad_key_lin = rotary_back(
        pair_local[:, :D].reshape(token_count, HEADS, HEAD_DIM), cosine, sine_table
    )
    grad_value_lin = pair_local[:, D:].reshape(token_count, HEADS, HEAD_DIM)
    grad_projected = (
        jnp.stack([grad_query_lin, grad_key_lin, grad_value_lin], axis=1)
        .reshape(token_count, 3 * D)
        .astype(jnp.bfloat16)
    )
    grad_qkv_weight = left_product(normed_one, grad_projected)
    grad_qkv_bias = jnp.sum(grad_projected.astype(jnp.float32), axis=0)
    grad_normed_one = right_product(grad_projected, attn_back[2])
    grad_gain_one = jnp.sum(grad_normed_one * scaled_one, axis=0)
    grad_bias_one = jnp.sum(grad_normed_one, axis=0)
    grad_tokens = grad_residual + norm_back(
        grad_normed_one, attn_back[0].astype(jnp.float32), scaled_one, inverse_one
    )
    attn_shards = (
        lax.psum_scatter(grad_gain_one, ("batch", "ctx"), scatter_dimension=0, tiled=True),
        lax.psum_scatter(grad_bias_one, ("batch", "ctx"), scatter_dimension=0, tiled=True),
        lax.psum_scatter(grad_qkv_weight, ("batch", "ctx"), scatter_dimension=0, tiled=True),
        lax.psum_scatter(grad_qkv_bias, ("batch", "ctx"), scatter_dimension=0, tiled=True),
        lax.psum_scatter(grad_out_weight, ("batch", "ctx"), scatter_dimension=0, tiled=True),
    )
    return (
        hidden_out[None],
        grad_tokens[None],
        attn_shards[0],
        attn_shards[1],
        attn_shards[2],
        attn_shards[3],
        attn_shards[4],
        mlp_shards[0],
        mlp_shards[1],
        mlp_shards[2],
        mlp_shards[3],
        mlp_shards[4],
    )

RUN = 128
PAIR = 2 * HEAD_DIM
VMEM_LIMIT = 48 * 1024 * 1024


def turn(values, tables):
    cosine, sine_up, sine_down = tables
    return (
        values * cosine
        + pltpu.roll(values, ROT // 2, 1) * sine_up
        + pltpu.roll(values, PAIR - ROT // 2, 1) * sine_down
    )


def turn_back(values, tables):
    cosine, sine_up, sine_down = tables
    return (
        values * cosine
        - pltpu.roll(values, ROT // 2, 1) * sine_up
        - pltpu.roll(values, PAIR - ROT // 2, 1) * sine_down
    )


def run_rows(runs, index):
    return pl.ds(pl.multiple_of(runs[index] * RUN, RUN), RUN)


def score_block(query, keys, start):
    scores = lax.dot_general(
        query, keys, (((1,), (1,)), ((), ())), preferred_element_type=jnp.float32
    )
    row = lax.broadcasted_iota(jnp.int32, scores.shape, 0) + start
    column = lax.broadcasted_iota(jnp.int32, scores.shape, 1)
    scores = jnp.where(column <= row, scores, NEGATIVE)
    weights = jnp.exp(scores - jnp.max(scores, axis=1, keepdims=True))
    return weights, jnp.sum(weights, axis=1, keepdims=True)


def head_lanes(values, head):
    lane = lax.broadcasted_iota(jnp.int32, values.shape, 1)
    return jnp.where((lane < HEAD_DIM) == (head == 0), values, jnp.zeros_like(values))


def attention_kernel(runs, q, k, v, cosine, sine_up, sine_down, out, q_kept, k_kept, v_kept):
    length = q.shape[0]
    for index in range(length // RUN):
        rows = run_rows(runs, index)
        place = slice(index * RUN, (index + 1) * RUN)
        tables = cosine[rows, :], sine_up[rows, :], sine_down[rows, :]
        q_kept[place, :] = turn(q[rows, :], tables).astype(jnp.bfloat16)
        k_kept[place, :] = turn(k[rows, :], tables).astype(jnp.bfloat16)
        v_kept[place, :] = v[rows, :].astype(jnp.bfloat16)
    step = 2 * RUN
    for index in range(length // step):
        seen = (index + 1) * step
        query = q_kept[index * step : seen, :]
        result = 0.0
        for head in (0, 1):
            weights, total = score_block(
                head_lanes(query, head) * 0.125, k_kept[:seen, :], index * step
            )
            summed = jnp.dot(
                weights.astype(jnp.bfloat16), v_kept[:seen, :], preferred_element_type=jnp.float32
            )
            result = result + head_lanes(summed / total, head)
        result = result.astype(jnp.bfloat16)
        out[run_rows(runs, 2 * index), :] = result[:RUN]
        out[run_rows(runs, 2 * index + 1), :] = result[RUN:]


def attention_back_kernel(
    runs, q, k, v, grad, cosine, sine_up, sine_down, q_out, k_out, v_out, k_sum, v_sum
):
    length = q.shape[0]
    step = 2 * RUN
    k_sum[...] = jnp.zeros_like(k_sum)
    v_sum[...] = jnp.zeros_like(v_sum)
    for index in range(length // step):
        seen = (index + 1) * step
        query = q[index * step : seen, :]
        pair = [run_rows(runs, 2 * index), run_rows(runs, 2 * index + 1)]
        grad_rows = jnp.concatenate([grad[rows, :] for rows in pair], axis=0)
        grad_query = 0.0
        for head in (0, 1):
            query_head = head_lanes(query, head) * 0.125
            grad_head = head_lanes(grad_rows, head)
            weights, total = score_block(query_head, k[:seen, :], index * step)
            weights = weights / total
            grad_weights = lax.dot_general(
                grad_head, v[:seen, :], (((1,), (1,)), ((), ())), preferred_element_type=jnp.float32
            )
            row_dot = jnp.sum(weights * grad_weights, axis=1, keepdims=True)
            grad_scores = (weights * (grad_weights - row_dot)).astype(jnp.bfloat16)
            grad_query = grad_query + head_lanes(
                jnp.dot(grad_scores, k[:seen, :], preferred_element_type=jnp.float32), head
            )
            k_sum[:seen, :] += left_product(grad_scores, query_head)
            v_sum[:seen, :] += left_product(weights.astype(jnp.bfloat16), grad_head)
        grad_query = grad_query * 0.125
        for part, rows in enumerate(pair):
            tables = cosine[rows, :], sine_up[rows, :], sine_down[rows, :]
            q_out[rows, :] = turn_back(
                grad_query[part * RUN : (part + 1) * RUN], tables
            ).astype(jnp.bfloat16)
    for index in range(length // RUN):
        rows = run_rows(runs, index)
        place = slice(index * RUN, (index + 1) * RUN)
        tables = cosine[rows, :], sine_up[rows, :], sine_down[rows, :]
        k_out[rows, :] = turn_back(k_sum[place, :], tables).astype(jnp.bfloat16)
        v_out[rows, :] = v_sum[place, :].astype(jnp.bfloat16)


def attention_forward(runs, projected, tables, width):
    length = projected.shape[0]
    pairs = width // PAIR
    column = lambda start: pl.BlockSpec((length, PAIR), lambda i, _: (0, i + start))
    whole = pl.BlockSpec((length, PAIR), lambda i, _: (0, 0))
    shape = jax.ShapeDtypeStruct((length, width), jnp.bfloat16)
    return pl.pallas_call(
        attention_kernel,
        out_shape=[shape] * 4,
        grid_spec=pltpu.PrefetchScalarGridSpec(
            num_scalar_prefetch=1,
            grid=(pairs,),
            in_specs=[column(0), column(pairs), column(2 * pairs)] + [whole] * 3,
            out_specs=[column(0)] * 4,
        ),
        compiler_params=pltpu.CompilerParams(vmem_limit_bytes=VMEM_LIMIT),
        cost_estimate=pl.CostEstimate(
            flops=6 * length * length * width,
            bytes_accessed=20 * length * width,
            transcendentals=2 * pairs * length * length,
        ),
        name="attention_forward",
    )(runs, projected, projected, projected, *tables)


def attention_backward(runs, kept, grad, tables):
    length, width = grad.shape
    column = pl.BlockSpec((length, PAIR), lambda i, _: (0, i))
    whole = pl.BlockSpec((length, PAIR), lambda i, _: (0, 0))
    shape = jax.ShapeDtypeStruct((length, width), jnp.bfloat16)
    return pl.pallas_call(
        attention_back_kernel,
        out_shape=[shape] * 3,
        grid_spec=pltpu.PrefetchScalarGridSpec(
            num_scalar_prefetch=1,
            grid=(width // PAIR,),
            in_specs=[column] * 4 + [whole] * 3,
            out_specs=[column] * 3,
            scratch_shapes=[pltpu.VMEM((length, PAIR), jnp.float32)] * 2,
        ),
        compiler_params=pltpu.CompilerParams(vmem_limit_bytes=VMEM_LIMIT),
        cost_estimate=pl.CostEstimate(
            flops=20 * length * length * width,
            bytes_accessed=14 * length * width,
            transcendentals=2 * width // PAIR * length * length,
        ),
        name="attention_backward",
    )(runs, *kept, grad, *tables)


def unit_moves(unit):
    moves = []
    for y in (0, 1):
        for x in (0, 1):
            for r in (0, 1):
                for q in (0, 1):
                    for parity in (0, 1):
                        whole = ((((y * 2 + x) * 2 + r) * 2 + q) * 2 + parity) * unit
                        moves.append((x, parity, whole, ((y * 2 + r) * 2 + q) * unit))
    return moves


def split_kernel(gate, up, out, wide, packed):
    rows, columns = gate.shape
    unit = columns // 32
    for half, weight in enumerate((gate, up)):
        wide[...] = weight[...].astype(jnp.float32)
        for x, parity, whole, place in unit_moves(unit):
            at = half * (columns // 4) + place
            packed[x, parity * rows : (parity + 1) * rows, at : at + unit] = wide[
                :, whole : whole + unit
            ]
    out[...] = packed[...].astype(jnp.bfloat16)


def join_kernel(first, second, gate, up, wide):
    rows, columns = gate.shape
    unit = columns // 32
    for x, part in enumerate((first, second)):
        wide[x] = part[...].astype(jnp.float32)
    for half, weight in enumerate((gate, up)):
        for x, parity, whole, place in unit_moves(unit):
            at = half * (columns // 4) + place
            weight[:, whole : whole + unit] = wide[
                x, parity * rows : (parity + 1) * rows, at : at + unit
            ]


def split_units(gate, up):
    rows, columns = gate.shape
    packed = (2, 2 * rows, columns // 2)
    return pl.pallas_call(
        split_kernel,
        out_shape=jax.ShapeDtypeStruct(packed, jnp.bfloat16),
        scratch_shapes=[
            pltpu.VMEM((rows, columns), jnp.float32),
            pltpu.VMEM(packed, jnp.float32),
        ],
        compiler_params=pltpu.CompilerParams(vmem_limit_bytes=VMEM_LIMIT),
        name="split_units",
    )(gate, up)


def join_units(first, second):
    rows, columns = first.shape[0] // 2, 2 * first.shape[1]
    shape = jax.ShapeDtypeStruct((rows, columns), jnp.float32)
    return pl.pallas_call(
        join_kernel,
        out_shape=[shape, shape],
        scratch_shapes=[pltpu.VMEM((2, *first.shape), jnp.float32)],
        compiler_params=pltpu.CompilerParams(vmem_limit_bytes=VMEM_LIMIT),
        name="join_units",
    )(first, second)


def pair_tables(places):
    cosine, sine_table = rotary_tables(places)
    cosine, sine_table = cosine[:, 0], sine_table[:, 0]
    first = jnp.arange(HEAD_DIM) < ROT // 2
    up = jnp.where(first, 0.0, sine_table)
    down = jnp.where(first, -sine_table, 0.0)
    return [jnp.concatenate([table, table], axis=1) for table in (cosine, up, down)]


def swap(values, axis, mask):
    return lax.ppermute(values, axis, [(i, i ^ mask) for i in range(lax.axis_size(axis))])


def add_low(left, right):
    return (left.astype(jnp.float32) + right.astype(jnp.float32)).astype(jnp.bfloat16)


def relative_four(parts):
    place = lax.axis_index("ctx")
    odd, high = place % 2 == 1, place // 2 == 1
    once = [jnp.where(odd, parts[j ^ 1], parts[j]) for j in range(4)]
    return [jnp.where(high, once[j ^ 2], once[j]) for j in range(4)]


def after(values, *earlier):
    return lax.optimization_barrier((values, earlier))[0]


def greet(place, last):
    barrier = pltpu.get_barrier_semaphore()
    for there, near in ((place > 0, place - 1), (place < last, place + 1)):

        @pl.when(there)
        def _():
            pl.semaphore_signal(
                barrier, inc=1, device_id={"ctx": near}, device_id_type=pl.DeviceIdType.MESH
            )

    peers = jnp.where(place > 0, 1, 0) + jnp.where(place < last, 1, 0)
    pl.semaphore_wait(barrier, peers)


def towards(source, target, send, receive, device):
    return pltpu.make_async_remote_copy(
        src_ref=source,
        dst_ref=target,
        send_sem=send,
        recv_sem=receive,
        device_id={"ctx": device},
        device_id_type=pl.DeviceIdType.MESH,
    )


def gather_kernel(own, out, local, send_up, receive_up, send_down, receive_down):
    place = lax.axis_index("ctx")
    last = out.shape[0] - 1
    greet(place, last)
    mine = pltpu.make_async_copy(own, out.at[place], local)
    mine.start()
    for step in range(last):
        up_from = jnp.maximum(place - step, 0)
        down_from = jnp.minimum(place + step, last)
        source_up = own if step == 0 else out.at[up_from]
        source_down = own if step == 0 else out.at[down_from]
        up = towards(
            source_up,
            out.at[up_from],
            send_up.at[step],
            receive_up.at[step],
            jnp.minimum(place + 1, last),
        )
        down = towards(
            source_down,
            out.at[down_from],
            send_down.at[step],
            receive_down.at[step],
            jnp.maximum(place - 1, 0),
        )

        @pl.when((place >= step) & (place < last))
        def _():
            up.start()

        @pl.when((place <= last - step) & (place > 0))
        def _():
            down.start()

        @pl.when(place >= step + 1)
        def _():
            up.wait_recv()

        @pl.when(place <= last - step - 1)
        def _():
            down.wait_recv()

        @pl.when((place >= step) & (place < last))
        def _():
            up.wait_send()

        @pl.when((place <= last - step) & (place > 0))
        def _():
            down.wait_send()

    mine.wait()


def gather_tokens(block, group):
    size = lax.axis_size("ctx")
    return pl.pallas_call(
        gather_kernel,
        out_shape=jax.ShapeDtypeStruct((size, *block.shape), block.dtype),
        in_specs=[pl.BlockSpec(memory_space=pl.ANY)],
        out_specs=pl.BlockSpec(memory_space=pl.ANY),
        scratch_shapes=[pltpu.SemaphoreType.DMA] + [pltpu.SemaphoreType.DMA((size - 1,))] * 4,
        compiler_params=pltpu.CompilerParams(collective_id=group, has_side_effects=True),
        cost_estimate=pl.CostEstimate(
            flops=0, bytes_accessed=500 * block.size, transcendentals=0
        ),
        name="gather_tokens",
    )(block)


def scatter_kernel(
    partial, out, sum_up, sum_down, in_up, in_down, send_up, receive_up, send_down, receive_down
):
    place = lax.axis_index("ctx")
    last = partial.shape[0] - 1
    greet(place, last)
    for step in range(last):
        up_to = jnp.minimum(place + last - step, last)
        down_to = jnp.maximum(place - last + step, 0)
        goes_up = (place <= step) & (place < last)
        goes_down = (place >= last - step) & (place > 0)

        @pl.when(goes_up)
        def _():
            sum_up[step] = partial[up_to]

        @pl.when(goes_down)
        def _():
            sum_down[step] = partial[down_to]

        if step > 0:

            @pl.when(goes_up & (place > 0))
            def _():
                sum_up[step] = add_low(sum_up[step], in_up[step - 1])

            @pl.when(goes_down & (place < last))
            def _():
                sum_down[step] = add_low(sum_down[step], in_down[step - 1])

        up = towards(
            sum_up.at[step],
            in_up.at[step],
            send_up.at[step],
            receive_up.at[step],
            jnp.minimum(place + 1, last),
        )
        down = towards(
            sum_down.at[step],
            in_down.at[step],
            send_down.at[step],
            receive_down.at[step],
            jnp.maximum(place - 1, 0),
        )

        @pl.when(goes_up)
        def _():
            up.start()

        @pl.when(goes_down)
        def _():
            down.start()

        if step == 0:
            out[...] = partial[place].astype(jnp.float32)

        @pl.when((place > 0) & (place - 1 <= step))
        def _():
            up.wait_recv()

        @pl.when((place < last) & (place + 1 >= last - step))
        def _():
            down.wait_recv()

        @pl.when(goes_up)
        def _():
            up.wait_send()

        @pl.when(goes_down)
        def _():
            down.wait_send()

    @pl.when(place > 0)
    def _():
        out[...] += in_up[last - 1].astype(jnp.float32)

    @pl.when(place < last)
    def _():
        out[...] += in_down[last - 1].astype(jnp.float32)


def scatter_tokens(partial, group):
    size = lax.axis_size("ctx")
    partial = partial.astype(jnp.bfloat16).reshape(size, -1, partial.shape[1])
    block = partial.shape[1:]
    buffer = pltpu.VMEM((size - 1, *block), jnp.bfloat16)
    return pl.pallas_call(
        scatter_kernel,
        out_shape=jax.ShapeDtypeStruct(block, jnp.float32),
        in_specs=[pl.BlockSpec(memory_space=pltpu.VMEM)],
        out_specs=pl.BlockSpec(memory_space=pltpu.VMEM),
        scratch_shapes=[buffer] * 4 + [pltpu.SemaphoreType.DMA((size - 1,))] * 4,
        compiler_params=pltpu.CompilerParams(
            collective_id=group, has_side_effects=True, vmem_limit_bytes=VMEM_LIMIT
        ),
        cost_estimate=pl.CostEstimate(
            flops=0, bytes_accessed=150 * partial.size, transcendentals=0
        ),
        name="scatter_tokens",
    )(partial)


def gather_small(values):
    every = values[None]
    for mask in (1, 2, 4):
        every = jnp.concatenate([every, swap(every, "batch", mask)], axis=0)
    return every


def scatter_small(vectors):
    own, place = lax.axis_index("batch"), lax.axis_index("ctx")
    index = jnp.arange(32)
    rest = jnp.take(vectors, ((index % 8) ^ own) * 4 + ((index // 8) ^ place), axis=0)
    for axis, mask in (("ctx", 2), ("ctx", 1), ("batch", 4), ("batch", 2), ("batch", 1)):
        middle = rest.shape[0] // 2
        rest = rest[:middle] + swap(rest[middle:], axis, mask)
    return rest[0]


def by_bit(bit, parts):
    return jnp.where(bit, parts[1], parts[0]), jnp.where(bit, parts[0], parts[1])


def quad_gather(block, between=None):
    half = block.shape[0] // 2
    from_x = swap(block, "batch", 2)
    from_z = swap(block, "ctx", 1)
    if between is not None:
        from_x, from_z = between((from_x, from_z))
    top = swap(from_z[:half], "batch", 2)
    low = swap(from_x[half:], "ctx", 1)
    return jnp.concatenate([block, from_x, from_z, top, low], axis=0)


def quad_scatter(partial, work=None):
    rows = partial.shape[0] // 4
    half = rows // 2
    low_bits = partial[rows:].astype(jnp.bfloat16)
    x_top, x_low, z_top, z_low, d_top, d_low = [
        low_bits[j * half : (j + 1) * half] for j in range(6)
    ]
    top = swap(jnp.concatenate([z_top, d_top], axis=0), "ctx", 1)
    low = swap(jnp.concatenate([x_low, d_low], axis=0), "batch", 2)
    result = None
    if work is not None:
        result = work()
        top, low = after((top, low), result)
    top_last = swap(add_low(x_top, top[half:]), "batch", 2)
    low_last = swap(add_low(z_low, low[half:]), "ctx", 1)
    first = jnp.concatenate([top[:half], low[:half]], axis=0).astype(jnp.float32)
    last = jnp.concatenate([top_last, low_last], axis=0).astype(jnp.float32)
    return partial[:rows] + first + last, result


def swap_block_order(values):
    size = values.shape[1] // 8
    order = (0, 2, 1, 3, 4, 6, 5, 7)
    return jnp.concatenate([values[:, j * size : (j + 1) * size] for j in order], axis=1)


SAME_X = [[0, 1, 4, 5], [2, 3, 6, 7]]


def split_columns(weight, unit):
    rows, columns = weight.shape
    pieces = weight.reshape(rows, columns // (4 * unit), 4, unit)
    return [pieces[:, :, j].reshape(rows, columns // 4) for j in range(4)]


def join_columns(parts, unit):
    rows, columns = parts[0].shape
    spread = jnp.stack([part.reshape(rows, columns // unit, unit) for part in parts], axis=2)
    return spread.reshape(rows, 4 * columns)


def body_chain(
    hidden_in,
    positions,
    norm1_gain,
    norm1_bias,
    w_qkv,
    b_qkv,
    w_out,
    norm2_gain,
    norm2_bias,
    w_gate,
    w_up,
    w_down,
    cotangent,
):
    place = lax.axis_index("ctx")
    members = HEADS // 4
    width = members * HEAD_DIM
    share = norm1_gain.shape[0]
    ff_unit = w_down.shape[0]
    ff_part = 8 * ff_unit
    tokens = hidden_in.shape[1]

    coarse, fine = jnp.divmod(positions[0], 256)
    small = gather_small(
        jnp.concatenate(
            [norm1_gain, norm1_bias, norm2_gain, norm2_bias, b_qkv]
            + [part.astype(jnp.bfloat16) for part in (coarse, fine)]
        )
    )
    kept_small = small.shape[1]
    extra_rows = -(-small.size // (16 * D)) * 16
    extra = jnp.pad(small.reshape(-1), (0, extra_rows * D - small.size)).reshape(-1, D)
    token_blocks = gather_tokens(jnp.concatenate([hidden_in[0], extra], axis=0), 0)
    arrived_tokens = token_blocks
    small = token_blocks[:, tokens:].reshape(4, -1)[:, : small.size].reshape(4, 8, kept_small)
    tokens_all = token_blocks[:, :tokens].reshape(4 * tokens, D)
    kept = kept_small - 2 * tokens
    places = small[:, 0, kept:].astype(jnp.float32).astype(jnp.int32)
    places = (places[:, :tokens] * 256 + places[:, tokens:]).reshape(-1)
    index = jnp.arange(32)
    index = index % 4 * 8 + ((index // 4) ^ lax.axis_index("batch"))
    small = jnp.take(small.reshape(32, kept_small), index, axis=0)[:, :kept]
    gain_one = small[:, :share].reshape(-1).astype(jnp.float32)
    bias_one = small[:, share : 2 * share].reshape(-1).astype(jnp.float32)
    gain_two = small[:, 2 * share : 3 * share].reshape(-1).astype(jnp.float32)
    bias_two = small[:, 3 * share : 4 * share].reshape(-1).astype(jnp.float32)
    qkv_bias = small[:, 4 * share :].reshape(3, members, 4, HEAD_DIM)
    qkv_bias = lax.dynamic_index_in_dim(qkv_bias, place, 2, keepdims=False)
    qkv_bias = qkv_bias.reshape(3 * width).astype(jnp.float32)

    def exchange(pieces):
        pieces = relative_four(pieces)
        return [pieces[0]] + [swap(pieces[m], "ctx", m) for m in (1, 2, 3)]

    def gather_rows(arrived):
        rows = jnp.concatenate(relative_four(arrived), axis=0)
        return lax.all_gather(rows, "batch", axis=0, tiled=True)

    def sum_rows(gradient):
        return lax.psum_scatter(gradient, "batch", scatter_dimension=0, tiled=True)

    def exchange_back(mine):
        arrived = exchange([mine[j * share : (j + 1) * share] for j in range(4)])
        return [part.astype(jnp.float32) for part in relative_four(arrived)]

    qkv_weight = gather_rows(exchange(split_columns(after(w_qkv, extra), HEAD_DIM)))
    out_weight = lax.all_gather(w_out, "batch", axis=0, tiled=True)

    x_bit = lax.axis_index("batch") // 2 % 2 == 1
    odd, high = place % 2 == 1, place // 2 == 1

    kept_x, sent_x = by_bit(x_bit, split_units(w_gate, w_up))
    came_x = swap(sent_x, "batch", 2)
    first_x, second_x = by_bit(x_bit, [kept_x, came_x])
    for_parity = by_bit(
        odd,
        [
            jnp.concatenate(
                [part[parity * share : (parity + 1) * share] for part in (first_x, second_x)],
                axis=0,
            )
            for parity in (0, 1)
        ],
    )
    for_parity, cot_own = after((for_parity, cotangent[0]), arrived_tokens)
    gate_pieces = [for_parity[0]] + [swap(for_parity[m % 2], "ctx", m) for m in (1, 2, 3)]
    tables = pair_tables(places)
    starts = places[::RUN] // RUN
    order = jnp.arange(starts.shape[0])
    runs = jnp.sum(jnp.where(starts[None, :] == order[:, None], order[None, :], 0), axis=1)
    runs = runs.astype(jnp.int32)
    scaled_all, inverse_all = norm_forward(tokens_all.astype(jnp.float32))
    scaled_one = lax.dynamic_slice_in_dim(scaled_all, place * tokens, tokens, axis=0)
    inverse_one = lax.dynamic_slice_in_dim(inverse_all, place * tokens, tokens, axis=0)
    normed_all = (scaled_all * gain_one + bias_one).astype(jnp.bfloat16)
    projected = jnp.dot(normed_all, qkv_weight, preferred_element_type=jnp.float32) + qkv_bias
    attended, *kept = attention_forward(runs, projected, tables, width)
    branch = jnp.dot(attended, out_weight, preferred_element_type=jnp.float32)
    branch = branch.astype(jnp.bfloat16)
    branch, gate_pieces = after((branch, gate_pieces), branch)
    branch = scatter_tokens(branch, 1)
    down_piece = after(swap(after(w_down, gate_pieces), "ctx", 2), branch)
    cot_quad = quad_gather(cot_own, lambda passed: after(passed, attended))
    gate_pieces = relative_four(gate_pieces)
    gate_up = lax.all_gather(
        jnp.concatenate(
            [
                gate_pieces[z][x * share : (x + 1) * share]
                for x in (0, 1)
                for z in range(4)
            ],
            axis=0,
        ),
        "batch",
        axis=0,
        tiled=True,
        axis_index_groups=SAME_X,
    )
    down = lax.all_gather(
        jnp.concatenate(by_bit(high, [w_down, down_piece]), axis=0),
        "batch",
        axis=0,
        tiled=True,
        axis_index_groups=SAME_X,
    )

    residual = hidden_in[0].astype(jnp.float32) + branch

    scaled_two, inverse_two = norm_forward(residual)
    normed_quad = quad_gather(
        swap_block_order((scaled_two * gain_two + bias_two).astype(jnp.bfloat16))
    )
    both = jnp.dot(normed_quad, gate_up, preferred_element_type=jnp.float32)
    gate_value, up_value = both[:, :ff_part], both[:, ff_part:]
    sigmoid_gate = jax.nn.sigmoid(gate_value)
    activated = gate_value * sigmoid_gate
    hidden = (activated * up_value).astype(jnp.bfloat16)
    grad_units = right_product(cot_quad, down)
    grad_gate = grad_units * up_value * sigmoid_gate * (1.0 + gate_value * (1.0 - sigmoid_gate))
    grad_both = jnp.concatenate([grad_gate, grad_units * activated], axis=1).astype(jnp.bfloat16)
    grad_normed_two, grad_gate_up = quad_scatter(
        right_product(grad_both, gate_up),
        lambda: (
            left_product(hidden, cot_quad).astype(jnp.bfloat16),
            left_product(normed_quad, grad_both).astype(jnp.bfloat16),
        ),
    )
    grad_down, grad_gate_up = grad_gate_up
    grad_normed_two = swap_block_order(grad_normed_two)

    def sum_quarter(gradient):
        return lax.psum_scatter(
            gradient, "batch", scatter_dimension=0, tiled=True, axis_index_groups=SAME_X
        )

    grad_down = sum_quarter(grad_down)
    grad_gate_up = sum_quarter(grad_gate_up)
    grad_gain_two = jnp.sum(grad_normed_two * scaled_two, axis=0)
    grad_bias_two = jnp.sum(grad_normed_two, axis=0)
    grad_residual = cotangent[0].astype(jnp.float32) + norm_back(
        grad_normed_two, gain_two, scaled_two, inverse_two
    )

    grad_branch = gather_tokens(grad_residual.astype(jnp.bfloat16), 2).reshape(4 * tokens, D)
    grad_attended = right_product(grad_branch, out_weight).astype(jnp.bfloat16)
    grad_attended, grad_gate_up = after((grad_attended, grad_gate_up), grad_branch)
    forth = jnp.dot(hidden, down, preferred_element_type=jnp.float32)
    forth, _ = quad_scatter(after(forth, grad_attended))
    grad_out = left_product(attended, grad_branch).astype(jnp.bfloat16)
    gate_rows = relative_four(
        [
            jnp.concatenate(
                [grad_gate_up[(4 * x + z) * share : (4 * x + z + 1) * share] for x in (0, 1)],
                axis=0,
            )
            for z in range(4)
        ]
    )
    gate_rows = [gate_rows[0]] + [swap(gate_rows[m], "ctx", m) for m in (1, 2, 3)]
    grad_out = sum_rows(after(grad_out, grad_down))
    grad_projected = jnp.concatenate(
        attention_backward(runs, kept, grad_attended, tables), axis=1
    )
    grad_projected, gate_rows, grad_out = after(
        (grad_projected, gate_rows, grad_out), grad_projected
    )
    gate_rows = by_bit(odd, [add_low(gate_rows[m], gate_rows[m + 2]) for m in (0, 1)])
    kept_x, sent_x = by_bit(
        x_bit,
        [
            jnp.concatenate([part[x * share : (x + 1) * share] for part in gate_rows], axis=0)
            for x in (0, 1)
        ],
    )
    came_x = swap(sent_x, "batch", 2)
    partial = right_product(grad_projected, qkv_weight)
    hidden_out = (residual + forth).astype(jnp.bfloat16)

    grad_down = after(grad_down, grad_projected)
    down_kept, down_sent = by_bit(high, [grad_down[:ff_unit], grad_down[ff_unit:]])
    down_came = swap(down_sent, "ctx", 2)

    grad_qkv = sum_rows(left_product(normed_all, grad_projected).astype(jnp.bfloat16))
    grad_qkv_bias = jnp.sum(grad_projected.astype(jnp.float32), axis=0)
    wide_bias = jnp.where(
        jnp.arange(4)[None, None, :, None] == place,
        grad_qkv_bias.reshape(3, members, 1, HEAD_DIM),
        0.0,
    )
    vectors = [
        jnp.sum(partial * scaled_all, axis=0),
        jnp.sum(partial, axis=0),
        grad_gain_two,
        grad_bias_two,
        wide_bias,
    ]
    vectors = jnp.concatenate([part.reshape(32, -1) for part in vectors], axis=1)
    grad_normed_one = scatter_tokens(partial, 1)
    summed = scatter_small(vectors)
    parts = by_bit(x_bit, [kept_x, came_x])
    gate_shard, up_shard = join_units(*parts)
    down_shard = down_kept.astype(jnp.float32) + down_came.astype(jnp.float32)
    grad_tokens = grad_residual + norm_back(grad_normed_one, gain_one, scaled_one, inverse_one)
    out_shard = grad_out.astype(jnp.float32)
    qkv_shard = join_columns(exchange_back(grad_qkv), HEAD_DIM)
    return (
        hidden_out[None],
        grad_tokens[None],
        summed[:share],
        summed[share : 2 * share],
        qkv_shard,
        summed[4 * share :],
        out_shard,
        summed[2 * share : 3 * share],
        summed[3 * share : 4 * share],
        gate_shard,
        up_shard,
        down_shard,
    )


def solution(mesh):
    placed = (
        P("batch", "ctx", None),
        P("batch", "ctx"),
        P(("batch", "ctx")),
        P(("batch", "ctx")),
        P(("batch", "ctx"), None),
        P(("batch", "ctx")),
        P(("batch", "ctx"), None),
        P(("batch", "ctx")),
        P(("batch", "ctx")),
        P(("batch", "ctx"), None),
        P(("batch", "ctx"), None),
        P(("batch", "ctx"), None),
        P("batch", "ctx", None),
    )
    chain_of_four = mesh.shape["batch"] == 8 and mesh.shape["ctx"] == 4
    return jax.shard_map(
        body_chain if chain_of_four else body,
        mesh=mesh,
        in_specs=placed,
        out_specs=(
            P("batch", "ctx", None),
            P("batch", "ctx", None),
            P(("batch", "ctx")),
            P(("batch", "ctx")),
            P(("batch", "ctx"), None),
            P(("batch", "ctx")),
            P(("batch", "ctx"), None),
            P(("batch", "ctx")),
            P(("batch", "ctx")),
            P(("batch", "ctx"), None),
            P(("batch", "ctx"), None),
            P(("batch", "ctx"), None),
        ),
        check_vma=False,
    )
```
